256 devices in a mesh: ra: 16 (over x, z_hi, core), rb: 16 (over y, z_lo).
Axes of the slice: x: 4, y: 4, z: 8 (z_hi: 2, z_lo: 4; z = z_hi * 4 + z_lo), core: 2. Of those that a mesh axis runs over, the one named last changes fastest.
Arguments:
- features_a: bfloat16 [32, 128, 1024], P('ra', 'rb'), may hold values from -600 to 600
- features_b: bfloat16 [32, 128, 1024], P('rb', 'ra'), may hold values from -600 to 600
- weight_one: bfloat16 [16, 81], replicated, may hold values from -16 to 16
- bias_one: float32 [16], replicated, may hold values from -3 to 3
- weight_two: bfloat16 [16, 81], replicated, may hold values from -0.25 to 0.25
- bias_two: float32 [1], replicated, may hold values from -3 to 3
Outputs:
- consensus: float32 [32, 128, 32, 128], P('ra', None, 'rb')
The draws below stay inside these ranges and needn't reach their ends.
All inputs are finite; a program needn't handle non-finite values.
Results may differ from the reference program's by a relative error of at most 0.0053.
Values may be sent and summed in bfloat16 or wider, within the bound.
A program may use at most 192 MiB of HBM per device.

```python
import math
import jax
import jax.numpy as jnp
from jax import lax

C = 1024
HID = 16
W = 128
HA = 32
HB = 32


def draw_grid(key, rows):
    key_noise, key_cell, key_chan = jax.random.split(key, 3)
    noise = jax.random.truncated_normal(key_noise, -5.0, 5.0, (rows, W, C), jnp.float32)
    channel = jnp.exp(jax.random.uniform(key_chan, (C,), jnp.float32, 0.0, math.log(10.0)))
    cell_scale = jnp.exp(jax.random.uniform(key_cell, (rows, W, 1), jnp.float32, 0.0, math.log(10.0)))
    return noise * cell_scale * channel


def draw_features_a(key, part):
    return draw_grid(jax.random.fold_in(key, 11), HA).astype(jnp.bfloat16)


def draw_features_b(key, part):
    return draw_grid(jax.random.fold_in(key, 23), HB).astype(jnp.bfloat16)


def gaussian(rng, dims, spread, bound, kind=jnp.bfloat16):
    array = jax.random.normal(rng, dims, jnp.float32) * spread
    return jnp.minimum(jnp.maximum(array, -bound), bound).astype(kind)


def setup_inputs(seed: int = 0) -> dict:
    arg_keys = jax.random.split(jax.random.key(seed), 7)
    return {
        "features_a": draw_features_a(jax.random.fold_in(arg_keys[6], 71), 0),
        "features_b": draw_features_b(jax.random.fold_in(arg_keys[6], 71), 0),
        "weight_one": gaussian(arg_keys[2], (HID, 81), 2.5, 16.0),
        "bias_one": gaussian(arg_keys[3], (HID,), 0.5, 3.0, jnp.float32),
        "weight_two": gaussian(arg_keys[4], (HID, 81), (HID * 40) ** -0.5, 0.25),
        "bias_two": gaussian(arg_keys[5], (1,), 0.5, 3.0, jnp.float32),
    }


def normalize(features):
    values = features.astype(jnp.float32)
    scale = lax.rsqrt(lax.optimization_barrier(jnp.sum(values * values, axis=-1, keepdims=True)) + 1e-06)
    return (values * scale).astype(jnp.bfloat16)

def first_layer(volume, weight_one, bias_one, out_rows, out_k):
    width_j = volume.shape[1] - 2
    width_l = volume.shape[3] - 2
    weights = weight_one.astype(jnp.float32)

    def one_row(row_start):
        block = lax.dynamic_slice_in_dim(volume, row_start, 3, 0)
        patches = jnp.stack([block[t_i, t_j:t_j + width_j, t_k:t_k + out_k, t_l:t_l + width_l] for t_i in range(3) for t_j in range(3) for t_k in range(3) for t_l in range(3)])
        before = lax.dot_general(weights, patches.astype(jnp.float32), (((1,), (0,)), ((), ())))
        return jax.nn.relu(before + bias_one[:, None, None, None])
    return lax.map(one_row, jnp.arange(out_rows, dtype=jnp.int32))

def second_layer(hidden_pad, weight_two, bias_two, out_rows, out_k):
    width_j = hidden_pad.shape[2] - 2
    width_l = hidden_pad.shape[4] - 2
    weights = weight_two.astype(jnp.float32)

    def one_row(row_start):
        total = jnp.zeros((width_j, out_k, width_l), jnp.float32)
        for t_i in range(3):
            plane = lax.dynamic_index_in_dim(hidden_pad, row_start + t_i, 0, keepdims=False)
            taps = lax.dot_general(weights[:, 27 * t_i:27 * t_i + 27], plane.astype(jnp.float32), (((0,), (0,)), ((), ())))
            for t_j in range(3):
                for t_k in range(3):
                    for t_l in range(3):
                        total = total + taps[9 * t_j + 3 * t_k + t_l, t_j:t_j + width_j, t_k:t_k + out_k, t_l:t_l + width_l]
        return jax.nn.relu(total + bias_two[0])
    return lax.map(one_row, jnp.arange(out_rows, dtype=jnp.int32))

def reference(features_a, features_b, weight_one, bias_one, weight_two, bias_two):
    norm_a = normalize(features_a)
    norm_b = normalize(features_b)
    rows_a, width_j, channels = norm_a.shape
    rows_b, width_l, _ = norm_b.shape
    corr = jnp.dot(norm_a.reshape(-1, channels), norm_b.reshape(-1, channels).T, preferred_element_type=jnp.float32)
    corr = corr.reshape(rows_a, width_j, rows_b, width_l).astype(jnp.bfloat16)
    padded = jnp.pad(corr, 1)
    hidden = first_layer(padded, weight_one, bias_one, rows_a, rows_b).astype(jnp.bfloat16)
    hidden_pad = jnp.pad(hidden, ((1, 1), (0, 0), (1, 1), (1, 1), (1, 1)))
    return second_layer(hidden_pad, weight_two, bias_two, rows_a, rows_b)
```

```python
import functools

import jax
import jax.numpy as jnp
import ml_dtypes
import numpy as np
from jax import lax
from jax.experimental import pallas as pl
from jax.experimental.pallas import tpu as pltpu
from jax.sharding import PartitionSpec as P

HID = 16
LANES = 128
COLS = 512
USED = 432


def first_selector():
    table = np.zeros((81, 16, COLS), np.float32)
    for io in range(4):
        for ko in range(4):
            for a in range(3):
                for b in range(3):
                    for c in range(3):
                        for d in range(3):
                            col = ((b * 3 + d) * 6 + ko + c) * 8 + io + a
                            table[27 * a + 9 * b + 3 * c + d, io * 4 + ko, col] = 1
    return table.reshape(81, 16 * COLS).astype(ml_dtypes.bfloat16)


def second_selector():
    taps = np.zeros((9, 72, 81), np.float32)
    places = np.zeros((9, 72, 256), np.float32)
    for a in range(3):
        for c in range(3):
            for b in range(3):
                for d in range(3):
                    for i in range(2):
                        for k in range(2):
                            row = (b * 3 + d) * 8 + i * 2 + k
                            taps[a * 3 + c, row, 27 * a + 9 * b + 3 * c + d] = 1
                            start = ((i + a) * 4 + k + c) * HID
                            places[a * 3 + c, row, start : start + HID] = 1
    return (
        taps.reshape(648, 81).astype(ml_dtypes.bfloat16),
        places.reshape(648, 256).astype(ml_dtypes.bfloat16),
    )


def row_selector():
    table = np.zeros((64, 48), np.float32)
    for jj in range(8):
        for ii in range(6):
            table[jj * 8 + ii, ii * 8 + jj] = 1
    return table.astype(ml_dtypes.bfloat16)


def channel_tiler():
    return np.tile(np.eye(HID, dtype=np.float32), (1, 16)).astype(ml_dtypes.bfloat16)


def normalized(ref):
    values = ref[...].astype(jnp.float32)
    scale = lax.rsqrt(jnp.sum(values * values, axis=-1, keepdims=True) + 1e-06)
    return (values * scale).reshape(16, values.shape[-1]).astype(jnp.bfloat16)


def in_range(index, count):
    return jnp.logical_and(index >= 0, index < count)


class Copies:
    def __init__(self, send_sem, recv_sem):
        self.send_sem, self.recv_sem = send_sem, recv_sem
        self.started = []

    def start(self, src, dst, device):
        n = len(self.started)
        copy = pltpu.make_async_remote_copy(
            src_ref=src,
            dst_ref=dst,
            send_sem=self.send_sem.at[n],
            recv_sem=self.recv_sem.at[n],
            device_id=device,
            device_id_type=pl.DeviceIdType.MESH,
        )
        copy.start()
        self.started.append(copy)
        return copy


N_COPIES = 95


def place(ra, rb):
    x, zh, c = lax.div(ra, 4), lax.rem(lax.div(ra, 2), 2), lax.rem(ra, 2)
    y, zl = lax.div(rb, 4), lax.rem(rb, 4)
    return x, zh, c, y, zl


def greet(ra, rb):
    x, zh, c, y, zl = place(ra, rb)
    step = 2 * c - 1
    outer = lax.rem(ra + step + 16, 16)
    partners = [(outer, rb), (ra - step, rb), ((x * 2 + 1 - zh) * 2 + c, rb)]
    partners += [(ra, y * 4 + lax.rem(zl + t, 4)) for t in (1, 2, 3)]
    partners += [(ra, lax.rem(rb + t, 16)) for t in (4, 12)]
    partners += [(ra, lax.rem(rb + t, 16)) for t in (1, 15)]
    partners += [(lax.rem(ra + t, 16), rb) for t in (4, 12)]
    barrier = pltpu.get_barrier_semaphore()
    for device in partners:
        pl.semaphore_signal(barrier, inc=1, device_id=device, device_id_type=pl.DeviceIdType.MESH)
    return barrier, len(partners)


def gather(ra, rb, a_rows, b_rows, send_sem, recv_sem, meanwhile):
    copies = Copies(send_sem, recv_sem)
    x, zh, c, y, zl = place(ra, rb)
    step = 2 * c - 1
    outer = (lax.rem(ra + step + 16, 16), rb)
    mate = (ra - step, rb)
    far = ((x * 2 + 1 - zh) * 2 + c, rb)
    right_y, left_y = (ra, lax.rem(rb + 4, 16)), (ra, lax.rem(rb + 12, 16))
    right_x, left_x = (lax.rem(ra + 4, 16), rb), (lax.rem(ra + 12, 16), rb)
    next_b, prev_b = (ra, lax.rem(rb + 1, 16)), (ra, lax.rem(rb + 15, 16))
    ro = 2 * c
    mate_slot = 2 - 2 * (1 - c)

    def mate_a(index, count=1):
        part = pl.ds(index, count)
        return copies.start(a_rows.at[1, part], a_rows.at[mate_slot, part], mate)

    def mate_b(q, index, count=1):
        part = pl.ds(index, count)
        return copies.start(b_rows.at[q, c, part], b_rows.at[q, c, part], mate)

    def chunk_a(slot, index):
        return a_rows.at[slot, index]

    def chunk_b(q, index):
        return b_rows.at[q, c, index]

    def to_y(slot, index):
        return [
            copies.start(chunk_a(slot, index), chunk_a(slot, index), d) for d in (right_y, left_y)
        ]

    def to_x(q, index):
        return [copies.start(chunk_b(q, index), chunk_b(q, index), d) for d in (right_x, left_x)]

    here, there = x * 2 + zh, x * 2 + 1 - zh
    columns = [y * 4 + lax.rem(zl + 4 - t, 4) for t in range(4)]

    def to_z(slot):
        return [
            copies.start(chunk_a(slot, rb), chunk_a(slot, rb), (ra, y * 4 + lax.rem(zl + t, 4)))
            for t in (1, 2, 3)
        ]

    def to_rb(index):
        return [
            copies.start(chunk_b(1, index), chunk_b(0, index), next_b),
            copies.start(chunk_b(1, index), chunk_b(2, index), prev_b),
        ]

    mates = []
    b_far = copies.start(chunk_b(1, here), chunk_b(1, here), far)
    a_outer = copies.start(chunk_a(1, rb), chunk_a(2 - ro, rb), outer)
    z_own = to_z(1)
    rb_own = to_rb(here)
    y_own = [to_y(1, rb)]
    x_own = [to_x(1, here)]
    mates.append(mate_a(rb))
    mates.append(mate_b(1, here))

    meanwhile()

    b_far.wait_recv()
    rb_far = to_rb(there)
    x_far = [to_x(1, there)]
    mates.append(mate_b(1, there))

    a_outer.wait_recv()
    z_outer = to_z(ro)
    y_outer = [to_y(ro, rb)]

    for q, copy in ((0, rb_own[0]), (2, rb_own[1])):
        copy.wait_recv()
        x_own.append(to_x(q, here))
        mates.append(mate_b(q, here))

    for t in (1, 2, 3):
        z_own[t - 1].wait_recv()
        y_own.append(to_y(1, columns[t]))
        mates.append(mate_a(columns[t]))

    for q, copy in ((0, rb_far[0]), (2, rb_far[1])):
        copy.wait_recv()
        x_far.append(to_x(q, there))
        mates.append(mate_b(q, there))

    for t in (1, 2, 3):
        z_outer[t - 1].wait_recv()
        y_outer.append(to_y(ro, columns[t]))

    on_left = lax.rem(x + 3, 4) * 2
    on_right = lax.rem(x + 1, 4) * 2
    x_on = []
    own_right = zh == 0
    for q in range(3):
        pairs = (x_own[(1, 0, 2)[q]], x_far[(1, 0, 2)[q]])
        for pair in pairs:
            for copy in pair:
                copy.wait_recv()
        x_on.append(copies.start(chunk_b(q, on_left), chunk_b(q, on_left), right_x))
        x_on.append(copies.start(chunk_b(q, on_right + 1), chunk_b(q, on_right + 1), left_x))
        mates.append(mate_b(q, on_left, 2))
        mates.append(mate_b(q, on_right, 2))
    del own_right

    left_col = [lax.rem(y + 3, 4) * 4 + lax.rem(zl + 4 - t, 4) for t in range(4)]
    right_col = [lax.rem(y + 1, 4) * 4 + lax.rem(zl + 4 - t, 4) for t in range(4)]
    y_on = []
    for t in range(4):
        y_own[t][0].wait_recv()
        y_on.append(copies.start(chunk_a(1, left_col[t]), chunk_a(1, left_col[t]), right_y))
        y_own[t][1].wait_recv()
    for side in (3, 1):
        mates.append(mate_a(lax.rem(y + side, 4) * 4, 4))
    for t in range(4):
        y_outer[t][1].wait_recv()
        y_on.append(copies.start(chunk_a(ro, right_col[t]), chunk_a(ro, right_col[t]), left_y))
        y_outer[t][0].wait_recv()
    across = lax.rem(x + 2, 4) * 2
    for n, copy in enumerate(x_on):
        copy.wait_recv()
        if n % 2 == 1:
            mates.append(mate_b(n // 2, across, 2))
    for copy in y_on[:4]:
        copy.wait_recv()
    mates.append(mate_a(lax.rem(y + 2, 4) * 4, 4))
    for copy in y_on[4:]:
        copy.wait_recv()
    for copy in mates:
        copy.wait_recv()
    assert len(copies.started) <= N_COPIES, len(copies.started)
    return copies


def weights(ra, rb, w1_ref, bias1_ref, w2_ref, sel1, taps2, places2, tiler, big1, bias_big, big2):
    f32 = jnp.float32
    bias = bias1_ref[...]
    w1 = w1_ref[...]
    for io in range(4):
        for ko in range(4):
            n = io * 4 + ko
            inside = jnp.logical_and(in_range(2 * ra - 1 + io, 32), in_range(2 * rb - 1 + ko, 32))
            inside = inside.astype(f32)
            block = jnp.dot(w1, sel1[:, n * COLS : (n + 1) * COLS], preferred_element_type=f32)
            big1[n * HID : (n + 1) * HID, :] = (block * inside).astype(jnp.bfloat16)
            bias_big[n * HID : (n + 1) * HID, :] = bias * inside
    spread = lax.dot_general(
        w2_ref[...], tiler[...], (((0,), (0,)), ((), ())), preferred_element_type=f32
    ).astype(jnp.bfloat16)
    terms = jnp.dot(taps2[...], spread, preferred_element_type=f32) * places2[...].astype(f32)
    total = terms[0:72]
    for n in range(1, 9):
        total = total + terms[72 * n : 72 * n + 72]
    big2[...] = total.astype(jnp.bfloat16)


def shifted(values, by):
    lane = lax.broadcasted_iota(jnp.int32, values.shape, values.ndim - 1)
    moved = pltpu.roll(values, (-by) % LANES, values.ndim - 1)
    return jnp.where(lane == (0 if by < 0 else LANES - 1), jnp.zeros_like(moved), moved)


def arrange(ra, rb, a_rows, b_rows, rows, a_perm, b_perm):
    f32 = jnp.float32
    row = lax.broadcasted_iota(jnp.int32, (64, 48), 0)
    inside = in_range(2 * ra - 2 + lax.rem(row, 8), 32)
    select = jnp.where(inside, rows[...].astype(f32), 0.0).astype(jnp.bfloat16)

    def one_a(n, _):
        part = jnp.concatenate([a_rows[r, n] for r in range(3)], axis=0)
        a_perm[pl.ds(pl.multiple_of(n * 64, 64), 64), :] = jnp.dot(
            select, part, preferred_element_type=f32
        ).astype(jnp.bfloat16)
        return 0

    lax.fori_loop(0, 16, one_a, 0)
    for q in range(3):
        valid = in_range(rb - 1 + q, 16)
        for n in range(8):
            both = [b_rows[q, c, n].astype(f32) for c in range(2)]
            for k in range(2):
                rows16 = jnp.concatenate([v[8 * k : 8 * k + 8] for v in both], axis=0)
                b_perm[2 * q + k, 16 * n : 16 * n + 16, :] = jnp.where(
                    valid, rows16, 0.0
                ).astype(jnp.bfloat16)


J_STEP = 32


def correlate(a_perm, b_perm, patches):
    f32 = jnp.float32
    zero = jnp.zeros((9, 16, LANES), jnp.bfloat16)
    patches[0] = zero
    patches[129] = zero

    def one(n, _):
        part = a_perm[pl.ds(pl.multiple_of(n * J_STEP * 8, J_STEP * 8), J_STEP * 8), :]
        for pair in range(3):
            both = []
            for k in range(2):
                corr = lax.dot_general(
                    part, b_perm[2 * pair + k], (((1,), (1,)), ((), ())), preferred_element_type=f32
                )
                both.append(corr.reshape(J_STEP, 8, LANES))
            tile = jnp.concatenate(both, axis=1)
            for s in range(3):
                moved = tile if s == 1 else shifted(tile, s - 1)
                patches[pl.ds(1 + n * J_STEP, J_STEP), s * 3 + pair] = moved.astype(jnp.bfloat16)
        return 0

    lax.fori_loop(0, 128 // J_STEP, one, 0)


UNROLL = 2


def layers(patches, big1, bias_big, big2, taps):
    f32 = jnp.float32
    zero = jnp.zeros((72, LANES), f32)
    taps[0] = zero
    taps[129] = zero

    def one(n, _):
        for u in range(UNROLL):
            j = (n * UNROLL + u) * 2
            left = patches[pl.ds(j, 3)].reshape(USED, LANES)
            right = patches[pl.ds(j + 1, 3)].reshape(USED, LANES)
            before = jnp.dot(
                big1[:, :USED], jnp.concatenate([left, right], axis=1), preferred_element_type=f32
            )
            bias = bias_big[...]
            hidden = jnp.maximum(before + jnp.concatenate([bias, bias], axis=1), 0.0)
            out = jnp.dot(big2[...], hidden.astype(jnp.bfloat16), preferred_element_type=f32)
            taps[j + 1] = out[:, :LANES]
            taps[j + 2] = out[:, LANES:]
        return 0

    lax.fori_loop(0, 64 // UNROLL, one, 0)


def finish(taps, bias2, out_ref):
    step = 16

    def one(n, _):
        start = n * step
        sums = []
        for d in range(3):
            total = None
            for b in range(3):
                row = (b * 3 + d) * 8
                part = taps[pl.ds(start + b, step), row : row + 8]
                total = part if total is None else total + part
            sums.append(total)
        value = sums[1] + shifted(sums[0], -1) + shifted(sums[2], 1)
        value = jnp.maximum(value + bias2, 0.0)
        out_ref[0, pl.ds(start, step)] = value[:, 0:2]
        out_ref[1, pl.ds(start, step)] = value[:, 2:4]
        return 0

    lax.fori_loop(0, 128 // step, one, 0)


def kernel(
    a_ref, b_ref, w1_ref, bias1_ref, w2_ref, bias2_ref, sel1, taps2, places2, tiler, rows,
    out_ref,
    a_rows, b_rows, a_perm, b_perm, patches, taps, big1, bias_big, big2, send_sem, recv_sem,
):
    ra, rb = lax.axis_index("ra"), lax.axis_index("rb")
    x, zh, c, _, _ = place(ra, rb)
    barrier, count = greet(ra, rb)
    a_rows[1, rb] = normalized(a_ref)
    b_rows[1, c, x * 2 + zh] = normalized(b_ref)
    pl.semaphore_wait(barrier, count)
    copies = gather(
        ra, rb, a_rows, b_rows, send_sem, recv_sem,
        functools.partial(
            weights, ra, rb, w1_ref, bias1_ref, w2_ref, sel1, taps2, places2, tiler,
            big1, bias_big, big2,
        ),
    )
    arrange(ra, rb, a_rows, b_rows, rows, a_perm, b_perm)
    correlate(a_perm, b_perm, patches)
    layers(patches, big1, bias_big, big2, taps)
    finish(taps, bias2_ref[0], out_ref)
    for copy in copies.started:
        copy.wait_send()


SEL1 = first_selector()
TAPS2, PLACES2 = second_selector()
ROWS = row_selector()
TILER = channel_tiler()


def compute_scratch(channels):
    bf16, f32 = jnp.bfloat16, jnp.float32
    return [
        pltpu.VMEM((3, 16, 16, channels), bf16),
        pltpu.VMEM((3, 2, 8, 16, channels), bf16),
        pltpu.VMEM((1024, channels), bf16),
        pltpu.VMEM((6, LANES, channels), bf16),
        pltpu.VMEM((130, 9, 16, LANES), bf16),
        pltpu.VMEM((130, 72, LANES), f32),
        pltpu.VMEM((256, COLS), bf16),
        pltpu.VMEM((256, LANES), f32),
        pltpu.VMEM((72, 256), bf16),
    ]


def per_device(features_a, features_b, weight_one, bias_one, weight_two, bias_two):
    channels = features_a.shape[-1]
    vmem = pl.BlockSpec(memory_space=pltpu.VMEM)
    bias_cols = jnp.broadcast_to(bias_one[:, None], (HID, LANES))
    return pl.pallas_call(
        kernel,
        out_shape=jax.ShapeDtypeStruct((2, LANES, 2, LANES), jnp.float32),
        in_specs=[vmem] * 5 + [pl.BlockSpec(memory_space=pltpu.SMEM)] + [vmem] * 5,
        out_specs=vmem,
        scratch_shapes=compute_scratch(channels)
        + [pltpu.SemaphoreType.DMA((N_COPIES,)), pltpu.SemaphoreType.DMA((N_COPIES,))],
        compiler_params=pltpu.CompilerParams(
            collective_id=0, has_side_effects=True, vmem_limit_bytes=48 * 1024 * 1024
        ),
        name="consensus",
    )(
        features_a, features_b, weight_one, bias_cols, weight_two, bias_two,
        SEL1, TAPS2, PLACES2, TILER, ROWS,
    )


def solution(mesh):
    return jax.shard_map(
        per_device,
        mesh=mesh,
        in_specs=(P("ra", "rb", None), P("rb", "ra", None), P(), P(), P(), P()),
        out_specs=P("ra", None, "rb", None),
        check_vma=False,
    )
```

```python
import jax
import jax.numpy as jnp
from jax import lax
from jax.experimental import pallas as pl
from jax.experimental.pallas import tpu as pltpu
from jax.sharding import PartitionSpec as P

HID = 16
LANES = 128
COLS = 512
USED = 432
CELLS = 24
HALF = 64
CHUNKS = 9


def steps(values, size, count):
    total = jnp.zeros_like(values)
    for n in range(1, count):
        total = total + (values >= n * size).astype(jnp.int32)
    return total


def iota(shape, axis):
    return lax.broadcasted_iota(jnp.int32, shape, axis)


def as_bf16(mask):
    return jnp.where(mask, 1.0, 0.0).astype(jnp.bfloat16)


def normalized(ref):
    values = ref[...].astype(jnp.float32)
    scale = lax.rsqrt(jnp.sum(values * values, axis=-1, keepdims=True) + 1e-06)
    return (values * scale).reshape(16, values.shape[-1]).astype(jnp.bfloat16)


def in_range(index, count):
    return jnp.logical_and(index >= 0, index < count)


class Copies:
    def __init__(self, send_sem, recv_sem):
        self.send_sem, self.recv_sem = send_sem, recv_sem
        self.started = []

    def start(self, src, dst, device, arrives=None, later=False):
        n = len(self.started)
        copy = pltpu.make_async_remote_copy(
            src_ref=src,
            dst_ref=dst,
            send_sem=self.send_sem.at[n],
            recv_sem=self.recv_sem.at[n if arrives is None else arrives],
            device_id=device,
            device_id_type=pl.DeviceIdType.MESH,
        )
        if later:
            return copy
        copy.start()
        self.started.append((copy, None))
        return copy

    def start_when(self, copy, when):
        pl.when(when)(copy.start)
        self.started.append((copy, when))

    def wait_send(self):
        for copy, when in self.started:
            if when is None:
                copy.wait_send()
            else:
                pl.when(when)(copy.wait_send)


N_COPIES = 100
CHAIN = N_COPIES


class Place:
    def __init__(self, ra, rb):
        self.ra, self.rb = ra, rb
        self.x, self.zh, self.c = lax.div(ra, 4), lax.rem(lax.div(ra, 2), 2), lax.rem(ra, 2)
        self.y, self.zl = lax.div(rb, 4), lax.rem(rb, 4)
        self.chip = lax.div(ra, 2)
        flipped = (self.x * 2 + 1 - self.zh) * 2 + self.c
        self.mate = (ra + 1 - 2 * self.c, rb)
        self.far = (flipped, rb)
        self.line = [(ra, self.y * 4 + lax.rem(self.zl + t, 4)) for t in (1, 2, 3)]
        self.right_y, self.left_y = (ra, lax.rem(rb + 4, 16)), (ra, lax.rem(rb + 12, 16))
        self.right_x, self.left_x = (lax.rem(ra + 4, 16), rb), (lax.rem(ra + 12, 16), rb)
        self.next_b = (jnp.where(self.zl == 3, flipped, ra), lax.rem(rb + 1, 16))
        self.prev_b = (jnp.where(self.zl == 0, flipped, ra), lax.rem(rb + 15, 16))
        self.outer = lax.rem(ra + 2 * self.c + 15, 16)


def greet(p):
    barrier = pltpu.get_barrier_semaphore()

    def signal(device):
        pl.semaphore_signal(barrier, inc=1, device_id=device, device_id_type=pl.DeviceIdType.MESH)

    partners = [p.mate, p.far, p.right_y, p.left_y, p.right_x, p.left_x, p.next_b, p.prev_b]
    for device in partners + p.line:
        signal(device)

    @pl.when(p.zl == 0)
    def _():
        signal((p.outer, p.y * 4 + 2))
        signal((p.outer, p.y * 4 + 3))

    @pl.when(p.zl == 3)
    def _():
        signal((p.outer, p.y * 4))
        signal((p.outer, p.y * 4 + 1))

    return barrier, len(partners) + len(p.line) + 1


def gather(p, a_rows, b_rows, send_sem, recv_sem, meanwhile, have_b):
    copies = Copies(send_sem, recv_sem)
    x, zh, c, y, zl, rb = p.x, p.zh, p.c, p.y, p.zl, p.rb
    so, oo = 1 + c, 3 * c

    def mate_a(slot, index, count=1):
        part = a_rows.at[slot, pl.ds(index, count)]
        return copies.start(part, part, p.mate)

    def mate_b(q, index, count=1):
        part = b_rows.at[q, c, pl.ds(index, count)]
        return copies.start(part, part, p.mate)

    def chunk_a(slot, index):
        return a_rows.at[slot, index]

    def chunk_b(q, index):
        return b_rows.at[q, c, index]

    def to_y(slot, index):
        mates_a.append(mate_a(slot, index))
        return [
            copies.start(chunk_a(slot, index), chunk_a(slot, index), d)
            for d in (p.right_y, p.left_y)
        ]

    def to_x(q, index):
        mates_b.append(mate_b(q, index))
        return [
            copies.start(chunk_b(q, index), chunk_b(q, index), d) for d in (p.right_x, p.left_x)
        ]

    def to_rb(index):
        return [
            copies.start(chunk_b(1, index), chunk_b(0, index), p.next_b),
            copies.start(chunk_b(1, index), chunk_b(2, index), p.prev_b),
        ]

    here, there = x * 2 + zh, x * 2 + 1 - zh
    mates_a, mates_b = [], []

    end = (p.outer, y * 4 + jnp.where(zl >= 2, 0, 3))
    copies.start(chunk_a(so, rb), chunk_a(3 - oo, rb), end, arrives=CHAIN + zl)
    b_far = copies.start(chunk_b(1, here), chunk_b(1, here), p.far)
    z_own = [copies.start(chunk_a(so, rb), chunk_a(so, rb), d) for d in p.line]
    rb_own = to_rb(here)
    y_own = [to_y(so, rb)]
    x_own = [to_x(1, here)]

    meanwhile()

    near = zl < 2
    y_outer = []

    def chain(source):
        column = y * 4 + source
        onward = jnp.where(source >= 2, zl + 1, zl - 1)
        chunk = chunk_a(oo, column)
        neighbour = (p.ra, y * 4 + lax.rem(onward + 4, 4))
        copy = copies.start(chunk, chunk, neighbour, arrives=CHAIN + source, later=True)
        copy.wait_recv()
        copies.start_when(copy, in_range(onward, 4))
        y_outer.append(to_y(oo, column))

    columns = [y * 4 + lax.rem(zl + 4 - t, 4) for t in range(4)]

    def line(t):
        z_own[t - 1].wait_recv()
        y_own.append(to_y(so, columns[t]))

    chain_order = [jnp.where(near, 3, 0), jnp.where(near, 2, 1), jnp.where(near, 0, 3), jnp.where(near, 1, 2)]
    from_prev = [jnp.where(zl == 0, there, here), jnp.where(zl == 0, here, there)]
    from_next = [jnp.where(zl == 3, there, here), jnp.where(zl == 3, here, there)]

    chain(chain_order[0])
    line(1)
    chain(chain_order[1])
    line(3)
    for q, copy, index in ((0, rb_own[0], from_prev[0]), (2, rb_own[1], from_next[0])):
        copy.wait_recv()
        x_own.append(to_x(q, index))
    line(2)
    b_far.wait_recv()
    rb_far = to_rb(there)
    x_far = [to_x(1, there)]

    left_col = [lax.rem(y + 3, 4) * 4 + lax.rem(zl + 4 - t, 4) for t in range(4)]
    order = (0, 1, 3, 2)
    y_on = []

    def own_on(m):
        y_own[m][0].wait_recv()
        chunk = chunk_a(so, left_col[order[m]])
        y_on.append(copies.start(chunk, chunk, p.right_y))

    own_on(0)
    chain(chain_order[2])
    chain(chain_order[3])
    own_on(1)
    for q, copy, index in ((0, rb_far[0], from_prev[1]), (2, rb_far[1], from_next[1])):
        copy.wait_recv()
        x_far.append(to_x(q, index))
    own_on(2)
    own_on(3)

    on_left, on_right = lax.rem(x + 3, 4) * 2, lax.rem(x + 1, 4) * 2
    x_on = []

    def b_on(m):
        q = (1, 0, 2)[m]
        for pair in (x_own[m], x_far[m]):
            for copy in pair:
                copy.wait_recv()
        for index, device in ((on_left, p.right_x), (on_right + 1, p.left_x)):
            x_on.append(copies.start(chunk_b(q, index), chunk_b(q, index), device))
        mates_b.append(mate_b(q, on_left, 2))
        mates_b.append(mate_b(q, on_right, 2))

    outer_on = []

    def a_on(m):
        y_outer[m][1].wait_recv()
        chunk = chunk_a(oo, lax.rem(y + 1, 4) * 4 + chain_order[m])
        outer_on.append(copies.start(chunk, chunk, p.left_y))

    b_on(0)
    a_on(0)
    a_on(1)
    b_on(1)
    b_on(2)
    a_on(2)
    a_on(3)
    for copy in y_own:
        copy[1].wait_recv()
    for copy in y_outer:
        copy[0].wait_recv()
    for slot in (so, oo):
        for side in (3, 1):
            mates_a.append(mate_a(slot, lax.rem(y + side, 4) * 4, 4))
    across = lax.rem(x + 2, 4) * 2
    for n, copy in enumerate(x_on):
        copy.wait_recv()
        if n % 2 == 1:
            mates_b.append(mate_b((1, 0, 2)[n // 2], across, 2))
    for slot, arrivals in ((so, y_on), (oo, outer_on)):
        for copy in arrivals:
            copy.wait_recv()
        mates_a.append(mate_a(slot, lax.rem(y + 2, 4) * 4, 4))
    for copy in mates_b:
        copy.wait_recv()
    have_b()
    for copy in mates_a:
        copy.wait_recv()
    return copies


def weights(p, w1_ref, bias1_ref, w2_ref, big1, bias_big, big2):
    f32, bf16 = jnp.float32, jnp.bfloat16
    channel = iota((HID, LANES), 0)
    bias = jnp.zeros((HID, LANES), f32)
    for o in range(HID):
        bias = jnp.where(channel == o, bias1_ref[o], bias)
    w1 = w1_ref[...]
    tap = iota((81, COLS), 0)
    col = iota((1, COLS), 1)
    group = steps(col, 48, 11)
    tap_j = steps(group, 3, 4)
    shift = group - 3 * tap_j
    rest = col - 48 * group
    ki = steps(rest, 8, 6)
    ii = rest - 8 * ki
    for io in range(6):
        for ko in range(4):
            n = io * 4 + ko
            inside = jnp.logical_and(in_range(4 * p.chip - 1 + io, 32), in_range(2 * p.rb - 1 + ko, 32))
            inside = inside.astype(f32)
            a, c = ii - io, ki - ko
            fits = jnp.logical_and(jnp.logical_and(a >= 0, a < 3), jnp.logical_and(c >= 0, c < 3))
            wanted = jnp.where(
                jnp.logical_and(fits, col < USED), 27 * a + 9 * tap_j + 3 * c + shift, -1
            )
            block = jnp.dot(w1, as_bf16(tap == wanted), preferred_element_type=f32)
            big1[n * HID : (n + 1) * HID, :] = (block * inside).astype(bf16)
            bias_big[n * HID : (n + 1) * HID, :] = bias * inside
    tile = as_bf16(iota((HID, CELLS * HID), 0) == jnp.bitwise_and(iota((HID, CELLS * HID), 1), HID - 1))
    spread = lax.dot_general(
        w2_ref[...], tile, (((0,), (0,)), ((), ())), preferred_element_type=f32
    ).astype(bf16)
    row = iota((72, 1), 0)
    group = jnp.right_shift(row, 3)
    tap_j = steps(group, 3, 3)
    shift = group - 3 * tap_j
    i = jnp.bitwise_and(jnp.right_shift(row, 1) + 2 * p.c, 3)
    k = jnp.bitwise_and(row, 1)
    cell = jnp.right_shift(iota((72, CELLS * HID), 1), 4)
    tap = iota((72, 81), 1)
    total = jnp.zeros((72, CELLS * HID), f32)
    for a in range(3):
        for c in range(3):
            wanted = 27 * a + 9 * tap_j + 3 * c + shift
            term = jnp.dot(as_bf16(tap == wanted), spread, preferred_element_type=f32)
            total = total + jnp.where(cell == (i + a) * 4 + k + c, term, 0.0)
    big2[...] = total.astype(bf16)


def shifted(values, by):
    lane = lax.broadcasted_iota(jnp.int32, values.shape, values.ndim - 1)
    moved = pltpu.roll(values, (-by) % LANES, values.ndim - 1)
    return jnp.where(lane == (0 if by < 0 else LANES - 1), jnp.zeros_like(moved), moved)


def arrange_a(p, a_rows, a_perm):
    row, col = iota((64, 64), 0), iota((64, 64), 1)
    ii, jj = jnp.bitwise_and(row, 7), jnp.right_shift(row, 3)
    inside = in_range(4 * p.chip - 2 + ii, 32)
    select = as_bf16(jnp.logical_and(inside, col == ii * 8 + jj))
    for n in range(CHUNKS):
        part = jnp.concatenate([a_rows[slot, 7 * p.c + n] for slot in range(4)], axis=0)
        a_perm[n * 64 : (n + 1) * 64, :] = jnp.dot(
            select, part, preferred_element_type=jnp.float32
        ).astype(jnp.bfloat16)


def arrange_b(p, b_rows, b_perm):
    for q in range(3):
        valid = in_range(p.rb - 1 + q, 16)
        for n in range(8):
            both = [b_rows[q, c, n].astype(jnp.float32) for c in range(2)]
            for k in range(2):
                rows16 = jnp.concatenate([v[8 * k : 8 * k + 8] for v in both], axis=0)
                b_perm[2 * q + k, 16 * n : 16 * n + 16, :] = jnp.where(
                    valid, rows16, 0.0
                ).astype(jnp.bfloat16)


J_STEP = 24
EDGE = 8


def correlate(p, a_perm, b_perm, patches):
    f32 = jnp.float32
    patches[pl.ds(CHUNKS * 8 * p.c, EDGE)] = jnp.zeros((EDGE, 9, 16, LANES), jnp.bfloat16)
    base = EDGE * (1 - p.c)
    for n in range(CHUNKS * 8 // J_STEP):
        part = a_perm[n * J_STEP * 8 : (n + 1) * J_STEP * 8, :]
        for pair in range(3):
            both = []
            for k in range(2):
                corr = lax.dot_general(
                    part, b_perm[2 * pair + k], (((1,), (1,)), ((), ())), preferred_element_type=f32
                )
                both.append(corr.reshape(J_STEP, 8, LANES))
            tile = jnp.concatenate(both, axis=1)
            for s in range(3):
                moved = tile if s == 1 else shifted(tile, s - 1)
                patches[pl.ds(base + n * J_STEP, J_STEP), s * 3 + pair] = moved.astype(jnp.bfloat16)


GROUP = 11
PAIRS = 33


def layers(p, patches, big1, bias_big, big2, hidden, taps):
    f32 = jnp.float32

    def one(n, _):
        for u in range(GROUP):
            j = (n * GROUP + u) * 2 + EDGE - 2
            left = patches[pl.ds(j, 3)].reshape(USED, LANES)
            right = patches[pl.ds(j + 1, 3)].reshape(USED, LANES)
            before = jnp.dot(
                big1[:, :USED], jnp.concatenate([left, right], axis=1), preferred_element_type=f32
            )
            bias = bias_big[...]
            hidden[u] = jnp.maximum(before + jnp.concatenate([bias, bias], axis=1), 0.0).astype(
                jnp.bfloat16
            )
        for u in range(GROUP):
            j = (n * GROUP + u) * 2
            out = jnp.dot(big2[...], hidden[u], preferred_element_type=f32)
            taps[j] = out[:, :LANES]
            taps[j + 1] = out[:, LANES:]
        return 0

    lax.fori_loop(0, PAIRS // GROUP, one, 0)
    taps[(2 * PAIRS - 1) * p.c] = jnp.zeros((72, LANES), f32)


def finish(taps, bias2, own, other):
    step = 16
    for n in range(HALF // step):
        start = n * step
        sums = []
        for d in range(3):
            total = None
            for b in range(3):
                row = (b * 3 + d) * 8
                part = taps[start + b : start + b + step, row : row + 8]
                total = part if total is None else total + part
            sums.append(total)
        value = sums[1] + shifted(sums[0], -1) + shifted(sums[2], 1)
        value = jnp.maximum(value + bias2, 0.0)
        for i in range(2):
            own[i, start : start + step] = value[:, 2 * i : 2 * i + 2]
            other[i, start : start + step] = value[:, 4 + 2 * i : 6 + 2 * i]


def kernel(
    a_hbm, b_hbm, w1_hbm, bias1_hbm, w2_hbm, bias2_hbm,
    out_hbm,
    a_ref, b_ref, w1_ref, w2_ref, bias1_ref, bias2_ref, load_sem,
    a_rows, b_rows, a_perm, b_perm, patches, taps, big1, bias_big, big2, hidden, own, other,
    send_sem, recv_sem,
):
    p = Place(lax.axis_index("ra"), lax.axis_index("rb"))
    barrier, count = greet(p)
    pairs = (
        (a_hbm, a_ref), (b_hbm, b_ref), (w1_hbm, w1_ref),
        (w2_hbm, w2_ref), (bias1_hbm, bias1_ref), (bias2_hbm, bias2_ref),
    )
    loads = [
        pltpu.make_async_copy(src, dst, load_sem.at[n]) for n, (src, dst) in enumerate(pairs)
    ]
    for load in loads:
        load.start()
    loads[0].wait()
    a_rows[1 + p.c, p.rb] = normalized(a_ref)
    loads[1].wait()
    b_rows[1, p.c, p.x * 2 + p.zh] = normalized(b_ref)
    pl.semaphore_wait(barrier, count)

    def meanwhile():
        for load in loads[2:]:
            load.wait()
        weights(p, w1_ref, bias1_ref, w2_ref, big1, bias_big, big2)

    def have_b():
        arrange_b(p, b_rows, b_perm)

    copies = gather(p, a_rows, b_rows, send_sem, recv_sem, meanwhile, have_b)
    arrange_a(p, a_rows, a_perm)
    correlate(p, a_perm, b_perm, patches)
    layers(p, patches, big1, bias_big, big2, hidden, taps)
    finish(taps, bias2_ref[0], own, other)
    columns = pl.ds(HALF * p.c, HALF)
    handed = copies.start(other, out_hbm.at[:, columns], p.mate)
    kept = pltpu.make_async_copy(own, out_hbm.at[:, columns], load_sem.at[0])
    kept.start()
    copies.wait_send()
    kept.wait()
    handed.wait_recv()
    assert len(copies.started) <= N_COPIES, len(copies.started)


def compute_scratch(channels):
    bf16, f32 = jnp.bfloat16, jnp.float32
    return [
        pltpu.VMEM((4, 16, 16, channels), bf16),
        pltpu.VMEM((3, 2, 8, 16, channels), bf16),
        pltpu.VMEM((CHUNKS * 64, channels), bf16),
        pltpu.VMEM((6, LANES, channels), bf16),
        pltpu.VMEM((CHUNKS * 8 + EDGE, 9, 16, LANES), bf16),
        pltpu.VMEM((2 * PAIRS, 72, LANES), f32),
        pltpu.VMEM((CELLS * HID, COLS), bf16),
        pltpu.VMEM((CELLS * HID, LANES), f32),
        pltpu.VMEM((72, CELLS * HID), bf16),
        pltpu.VMEM((GROUP, CELLS * HID, 256), bf16),
        pltpu.VMEM((2, HALF, 2, LANES), f32),
        pltpu.VMEM((2, HALF, 2, LANES), f32),
    ]


def per_device(features_a, features_b, weight_one, bias_one, weight_two, bias_two):
    channels = features_a.shape[-1]
    arguments = (features_a, features_b, weight_one, bias_one, weight_two, bias_two)
    vmem = [pltpu.VMEM(v.shape, v.dtype) for v in (features_a, features_b, weight_one, weight_two)]
    smem = [pltpu.SMEM(v.shape, v.dtype) for v in (bias_one, bias_two)]
    return pl.pallas_call(
        kernel,
        out_shape=jax.ShapeDtypeStruct((2, LANES, 2, LANES), jnp.float32),
        in_specs=[pl.BlockSpec(memory_space=pl.ANY)] * 6,
        out_specs=pl.BlockSpec(memory_space=pl.ANY),
        scratch_shapes=vmem
        + smem
        + [pltpu.SemaphoreType.DMA((6,))]
        + compute_scratch(channels)
        + [pltpu.SemaphoreType.DMA((N_COPIES,)), pltpu.SemaphoreType.DMA((N_COPIES + 4,))],
        compiler_params=pltpu.CompilerParams(
            collective_id=0, has_side_effects=True, vmem_limit_bytes=60 * 1024 * 1024
        ),
        name="consensus",
    )(*arguments)


def solution(mesh):
    return jax.shard_map(
        per_device,
        mesh=mesh,
        in_specs=(P("ra", "rb", None), P("rb", "ra", None), P(), P(), P(), P()),
        out_specs=P("ra", None, "rb", None),
        check_vma=False,
    )
```

```python
import jax
import jax.numpy as jnp
from jax import lax
from jax.experimental import pallas as pl
from jax.experimental.pallas import tpu as pltpu
from jax.sharding import PartitionSpec as P

HID = 16
LANES = 128
COLS = 512
USED = 432
CELLS = 24
HALF = 64
CHUNKS = 9


def steps(values, size, count):
    total = jnp.zeros_like(values)
    for n in range(1, count):
        total = total + (values >= n * size).astype(jnp.int32)
    return total


def iota(shape, axis):
    return lax.broadcasted_iota(jnp.int32, shape, axis)


def as_bf16(mask):
    return jnp.where(mask, 1.0, 0.0).astype(jnp.bfloat16)


def normalized(ref):
    values = ref[...].astype(jnp.float32)
    scale = lax.rsqrt(jnp.sum(values * values, axis=-1, keepdims=True) + 1e-06)
    return (values * scale).reshape(16, values.shape[-1]).astype(jnp.bfloat16)


def in_range(index, count):
    return jnp.logical_and(index >= 0, index < count)


class Copies:
    def __init__(self, send_sem, recv_sem):
        self.send_sem, self.recv_sem = send_sem, recv_sem
        self.started, self.waiting = [], []

    def start(self, src, dst, device, arrives=None, later=False):
        n = len(self.started)
        copy = pltpu.make_async_remote_copy(
            src_ref=src,
            dst_ref=dst,
            send_sem=self.send_sem.at[n],
            recv_sem=self.recv_sem.at[n if arrives is None else arrives],
            device_id=device,
            device_id_type=pl.DeviceIdType.MESH,
        )
        if later:
            return copy
        copy.start()
        self.started.append(copy)
        self.waiting.append((copy, None))
        return copy

    def start_when(self, copy, when):
        pl.when(when)(copy.start)
        self.started.append(copy)
        self.waiting.append((copy, when))

    def wait_send(self):
        started, self.waiting = self.waiting, []
        for copy, when in started:
            if when is None:
                copy.wait_send()
            else:
                pl.when(when)(copy.wait_send)


N_COPIES = 100
CHAIN = N_COPIES


class Place:
    def __init__(self, ra, rb):
        self.ra, self.rb = ra, rb
        self.x, self.zh, self.c = lax.div(ra, 4), lax.rem(lax.div(ra, 2), 2), lax.rem(ra, 2)
        self.y, self.zl = lax.div(rb, 4), lax.rem(rb, 4)
        self.chip = lax.div(ra, 2)
        flipped = (self.x * 2 + 1 - self.zh) * 2 + self.c
        self.mate = (ra + 1 - 2 * self.c, rb)
        self.far = (flipped, rb)
        self.line = [(ra, self.y * 4 + lax.rem(self.zl + t, 4)) for t in (1, 2, 3)]
        self.right_y, self.left_y = (ra, lax.rem(rb + 4, 16)), (ra, lax.rem(rb + 12, 16))
        self.right_x, self.left_x = (lax.rem(ra + 4, 16), rb), (lax.rem(ra + 12, 16), rb)
        self.next_b = (jnp.where(self.zl == 3, flipped, ra), lax.rem(rb + 1, 16))
        self.prev_b = (jnp.where(self.zl == 0, flipped, ra), lax.rem(rb + 15, 16))
        self.outer = lax.rem(ra + 2 * self.c + 15, 16)


def greet(p):
    barrier = pltpu.get_barrier_semaphore()

    def signal(device):
        pl.semaphore_signal(barrier, inc=1, device_id=device, device_id_type=pl.DeviceIdType.MESH)

    partners = [p.mate, p.far, p.right_y, p.left_y, p.right_x, p.left_x, p.next_b, p.prev_b]
    for device in partners + p.line:
        signal(device)

    @pl.when(p.zl == 0)
    def _():
        signal((p.outer, p.y * 4 + 2))
        signal((p.outer, p.y * 4 + 3))

    @pl.when(p.zl == 3)
    def _():
        signal((p.outer, p.y * 4))
        signal((p.outer, p.y * 4 + 1))

    return barrier, len(partners) + len(p.line) + 1


def gather(p, a_rows, b_rows, send_sem, recv_sem, meanwhile, have_b):
    copies = Copies(send_sem, recv_sem)
    x, zh, c, y, zl, rb = p.x, p.zh, p.c, p.y, p.zl, p.rb
    so, oo = 1 + c, 3 * c

    def mate_a(slot, index, count=1):
        part = a_rows.at[slot, pl.ds(index, count)]
        return copies.start(part, part, p.mate)

    def mate_b(q, index, count=1):
        part = b_rows.at[q, c, pl.ds(index, count)]
        return copies.start(part, part, p.mate)

    def chunk_a(slot, index):
        return a_rows.at[slot, index]

    def chunk_b(q, index):
        return b_rows.at[q, c, index]

    def to_y(slot, index):
        mates_a.append(mate_a(slot, index))
        return [
            copies.start(chunk_a(slot, index), chunk_a(slot, index), d)
            for d in (p.right_y, p.left_y)
        ]

    def to_x(q, index):
        mates_b.append(mate_b(q, index))
        return [
            copies.start(chunk_b(q, index), chunk_b(q, index), d) for d in (p.right_x, p.left_x)
        ]

    def to_rb(index):
        return [
            copies.start(chunk_b(1, index), chunk_b(0, index), p.next_b),
            copies.start(chunk_b(1, index), chunk_b(2, index), p.prev_b),
        ]

    here, there = x * 2 + zh, x * 2 + 1 - zh
    mates_a, mates_b = [], []

    end = (p.outer, y * 4 + jnp.where(zl >= 2, 0, 3))
    copies.start(chunk_a(so, rb), chunk_a(3 - oo, rb), end, arrives=CHAIN + zl)
    b_far = copies.start(chunk_b(1, here), chunk_b(1, here), p.far)
    z_own = [copies.start(chunk_a(so, rb), chunk_a(so, rb), d) for d in p.line]
    rb_own = to_rb(here)
    y_own = [to_y(so, rb)]
    x_own = [to_x(1, here)]

    meanwhile()

    near = zl < 2
    y_outer = []

    def chain(source):
        column = y * 4 + source
        onward = jnp.where(source >= 2, zl + 1, zl - 1)
        chunk = chunk_a(oo, column)
        neighbour = (p.ra, y * 4 + lax.rem(onward + 4, 4))
        copy = copies.start(chunk, chunk, neighbour, arrives=CHAIN + source, later=True)
        copy.wait_recv()
        copies.start_when(copy, in_range(onward, 4))
        y_outer.append(to_y(oo, column))

    columns = [y * 4 + lax.rem(zl + 4 - t, 4) for t in range(4)]

    def line(t):
        z_own[t - 1].wait_recv()
        y_own.append(to_y(so, columns[t]))

    chain_order = [jnp.where(near, 3, 0), jnp.where(near, 2, 1), jnp.where(near, 0, 3), jnp.where(near, 1, 2)]
    from_prev = [jnp.where(zl == 0, there, here), jnp.where(zl == 0, here, there)]
    from_next = [jnp.where(zl == 3, there, here), jnp.where(zl == 3, here, there)]

    chain(chain_order[0])
    line(1)
    chain(chain_order[1])
    line(3)
    for q, copy, index in ((0, rb_own[0], from_prev[0]), (2, rb_own[1], from_next[0])):
        copy.wait_recv()
        x_own.append(to_x(q, index))
    line(2)
    b_far.wait_recv()
    rb_far = to_rb(there)
    x_far = [to_x(1, there)]

    left_col = [lax.rem(y + 3, 4) * 4 + lax.rem(zl + 4 - t, 4) for t in range(4)]
    order = (0, 1, 3, 2)
    y_on = []

    def own_on(m):
        y_own[m][0].wait_recv()
        chunk = chunk_a(so, left_col[order[m]])
        y_on.append(copies.start(chunk, chunk, p.right_y))

    own_on(0)
    chain(chain_order[2])
    chain(chain_order[3])
    own_on(1)
    for q, copy, index in ((0, rb_far[0], from_prev[1]), (2, rb_far[1], from_next[1])):
        copy.wait_recv()
        x_far.append(to_x(q, index))
    own_on(2)
    own_on(3)

    on_left, on_right = lax.rem(x + 3, 4) * 2, lax.rem(x + 1, 4) * 2
    x_on = []

    def b_on(m):
        q = (1, 0, 2)[m]
        for pair in (x_own[m], x_far[m]):
            for copy in pair:
                copy.wait_recv()
        for index, device in ((on_left, p.right_x), (on_right + 1, p.left_x)):
            x_on.append(copies.start(chunk_b(q, index), chunk_b(q, index), device))
        mates_b.append(mate_b(q, on_left, 2))
        mates_b.append(mate_b(q, on_right, 2))

    outer_on = []

    def a_on(m):
        y_outer[m][1].wait_recv()
        chunk = chunk_a(oo, lax.rem(y + 1, 4) * 4 + chain_order[m])
        outer_on.append(copies.start(chunk, chunk, p.left_y))

    b_on(0)
    a_on(0)
    a_on(1)
    b_on(1)
    b_on(2)
    a_on(2)
    a_on(3)
    for copy in y_own:
        copy[1].wait_recv()
    for copy in y_outer:
        copy[0].wait_recv()
    for slot in (so, oo):
        for side in (3, 1):
            mates_a.append(mate_a(slot, lax.rem(y + side, 4) * 4, 4))
    across = lax.rem(x + 2, 4) * 2
    for n, copy in enumerate(x_on):
        copy.wait_recv()
        if n % 2 == 1:
            mates_b.append(mate_b((1, 0, 2)[n // 2], across, 2))
    for slot, arrivals in ((so, y_on), (oo, outer_on)):
        for copy in arrivals:
            copy.wait_recv()
        mates_a.append(mate_a(slot, lax.rem(y + 2, 4) * 4, 4))
    copies.wait_send()
    for copy in mates_b:
        copy.wait_recv()
    have_b()
    for copy in mates_a:
        copy.wait_recv()
    return copies


def weights(p, w1_ref, bias1_ref, w2_ref, big1, bias_big, big2):
    f32, bf16 = jnp.float32, jnp.bfloat16
    channel = iota((HID, LANES), 0)
    bias = jnp.zeros((HID, LANES), f32)
    for o in range(HID):
        bias = jnp.where(channel == o, bias1_ref[o], bias)
    w1 = w1_ref[...]
    tap = iota((81, COLS), 0)
    col = iota((1, COLS), 1)
    group = steps(col, 48, 11)
    tap_j = steps(group, 3, 4)
    shift = group - 3 * tap_j
    rest = col - 48 * group
    ki = steps(rest, 8, 6)
    ii = rest - 8 * ki
    for io in range(6):
        for ko in range(4):
            n = io * 4 + ko
            inside = jnp.logical_and(in_range(4 * p.chip - 1 + io, 32), in_range(2 * p.rb - 1 + ko, 32))
            inside = inside.astype(f32)
            a, c = ii - io, ki - ko
            fits = jnp.logical_and(jnp.logical_and(a >= 0, a < 3), jnp.logical_and(c >= 0, c < 3))
            wanted = jnp.where(
                jnp.logical_and(fits, col < USED), 27 * a + 9 * tap_j + 3 * c + shift, -1
            )
            block = jnp.dot(w1, as_bf16(tap == wanted), preferred_element_type=f32)
            big1[n * HID : (n + 1) * HID, :] = (block * inside).astype(bf16)
            bias_big[n * HID : (n + 1) * HID, :] = bias * inside
    tile = as_bf16(iota((HID, CELLS * HID), 0) == jnp.bitwise_and(iota((HID, CELLS * HID), 1), HID - 1))
    spread = lax.dot_general(
        w2_ref[...], tile, (((0,), (0,)), ((), ())), preferred_element_type=f32
    ).astype(bf16)
    row = iota((72, 1), 0)
    group = jnp.right_shift(row, 3)
    tap_j = steps(group, 3, 3)
    shift = group - 3 * tap_j
    i = jnp.bitwise_and(jnp.right_shift(row, 1) + 2 * p.c, 3)
    k = jnp.bitwise_and(row, 1)
    cell = jnp.right_shift(iota((72, CELLS * HID), 1), 4)
    tap = iota((72, 81), 1)
    total = jnp.zeros((72, CELLS * HID), f32)
    for a in range(3):
        for c in range(3):
            wanted = 27 * a + 9 * tap_j + 3 * c + shift
            term = jnp.dot(as_bf16(tap == wanted), spread, preferred_element_type=f32)
            total = total + jnp.where(cell == (i + a) * 4 + k + c, term, 0.0)
    big2[...] = total.astype(bf16)


def shifted(values, by):
    lane = lax.broadcasted_iota(jnp.int32, values.shape, values.ndim - 1)
    moved = pltpu.roll(values, (-by) % LANES, values.ndim - 1)
    return jnp.where(lane == (0 if by < 0 else LANES - 1), jnp.zeros_like(moved), moved)


def arrange_a(p, a_rows, a_perm):
    row, col = iota((64, 64), 0), iota((64, 64), 1)
    ii, jj = jnp.bitwise_and(row, 7), jnp.right_shift(row, 3)
    inside = in_range(4 * p.chip - 2 + ii, 32)
    select = as_bf16(jnp.logical_and(inside, col == ii * 8 + jj))
    for n in range(CHUNKS):
        part = jnp.concatenate([a_rows[slot, 7 * p.c + n] for slot in range(4)], axis=0)
        a_perm[n * 64 : (n + 1) * 64, :] = jnp.dot(
            select, part, preferred_element_type=jnp.float32
        ).astype(jnp.bfloat16)


def arrange_b(p, b_rows, b_perm):
    for q in range(3):
        valid = in_range(p.rb - 1 + q, 16)
        for n in range(8):
            both = [b_rows[q, c, n].astype(jnp.float32) for c in range(2)]
            for k in range(2):
                rows16 = jnp.concatenate([v[8 * k : 8 * k + 8] for v in both], axis=0)
                b_perm[2 * q + k, 16 * n : 16 * n + 16, :] = jnp.where(
                    valid, rows16, 0.0
                ).astype(jnp.bfloat16)


J_STEP = 24
EDGE = 8


def correlate(p, a_perm, b_perm, patches):
    f32 = jnp.float32
    patches[pl.ds(CHUNKS * 8 * p.c, EDGE)] = jnp.zeros((EDGE, 9, 16, LANES), jnp.bfloat16)
    base = EDGE * (1 - p.c)
    for n in range(CHUNKS * 8 // J_STEP):
        part = a_perm[n * J_STEP * 8 : (n + 1) * J_STEP * 8, :]
        for pair in range(3):
            both = []
            for k in range(2):
                corr = lax.dot_general(
                    part, b_perm[2 * pair + k], (((1,), (1,)), ((), ())), preferred_element_type=f32
                )
                both.append(corr.reshape(J_STEP, 8, LANES))
            tile = jnp.concatenate(both, axis=1)
            for s in range(3):
                moved = tile if s == 1 else shifted(tile, s - 1)
                patches[pl.ds(base + n * J_STEP, J_STEP), s * 3 + pair] = moved.astype(jnp.bfloat16)


GROUP = 33
PAIRS = 33


def layers(p, patches, big1, bias_big, big2, hidden, taps):
    f32 = jnp.float32

    def one(n, _):
        for u in range(GROUP):
            j = (n * GROUP + u) * 2 + EDGE - 2
            left = patches[pl.ds(j, 3)].reshape(USED, LANES)
            right = patches[pl.ds(j + 1, 3)].reshape(USED, LANES)
            before = jnp.dot(
                big1[:, :USED], jnp.concatenate([left, right], axis=1), preferred_element_type=f32
            )
            bias = bias_big[...]
            hidden[u] = jnp.maximum(before + jnp.concatenate([bias, bias], axis=1), 0.0).astype(
                jnp.bfloat16
            )
        for u in range(GROUP):
            j = (n * GROUP + u) * 2
            out = jnp.dot(big2[...], hidden[u], preferred_element_type=f32)
            taps[j] = out[:, :LANES]
            taps[j + 1] = out[:, LANES:]
        return 0

    lax.fori_loop(0, PAIRS // GROUP, one, 0)
    taps[(2 * PAIRS - 1) * p.c] = jnp.zeros((72, LANES), f32)


def finish(taps, bias2, own, other):
    step = 16
    for n in range(HALF // step):
        start = n * step
        sums = []
        for d in range(3):
            total = None
            for b in range(3):
                row = (b * 3 + d) * 8
                part = taps[start + b : start + b + step, row : row + 8]
                total = part if total is None else total + part
            sums.append(total)
        value = sums[1] + shifted(sums[0], -1) + shifted(sums[2], 1)
        value = jnp.maximum(value + bias2, 0.0)
        for i in range(2):
            rows = slice(2 * start, 2 * (start + step))
            own[i, rows] = value[:, 2 * i : 2 * i + 2].reshape(2 * step, LANES)
            other[i, rows] = value[:, 4 + 2 * i : 6 + 2 * i].reshape(2 * step, LANES)


def kernel(
    a_hbm, b_hbm, w1_hbm, bias1_hbm, w2_hbm, bias2_hbm,
    out_hbm,
    a_ref, b_ref, w1_ref, w2_ref, bias1_ref, bias2_ref, load_sem,
    a_rows, b_rows, a_perm, b_perm, patches, taps, big1, bias_big, big2, hidden, own, other,
    send_sem, recv_sem,
):
    p = Place(lax.axis_index("ra"), lax.axis_index("rb"))
    barrier, count = greet(p)
    pairs = (
        (a_hbm, a_ref), (b_hbm, b_ref), (w1_hbm, w1_ref),
        (w2_hbm, w2_ref), (bias1_hbm, bias1_ref), (bias2_hbm, bias2_ref),
    )
    loads = [
        pltpu.make_async_copy(src, dst, load_sem.at[n]) for n, (src, dst) in enumerate(pairs)
    ]
    for load in loads:
        load.start()
    loads[0].wait()
    a_rows[1 + p.c, p.rb] = normalized(a_ref)
    loads[1].wait()
    b_rows[1, p.c, p.x * 2 + p.zh] = normalized(b_ref)
    pl.semaphore_wait(barrier, count)

    def meanwhile():
        for load in loads[2:]:
            load.wait()
        weights(p, w1_ref, bias1_ref, w2_ref, big1, bias_big, big2)

    def have_b():
        arrange_b(p, b_rows, b_perm)

    copies = gather(p, a_rows, b_rows, send_sem, recv_sem, meanwhile, have_b)
    arrange_a(p, a_rows, a_perm)
    correlate(p, a_perm, b_perm, patches)
    layers(p, patches, big1, bias_big, big2, hidden, taps)
    finish(taps, bias2_ref[0], own, other)
    columns = pl.ds(2 * HALF * p.c, 2 * HALF)
    handed = copies.start(other, out_hbm.at[:, columns], p.mate)
    kept = pltpu.make_async_copy(own, out_hbm.at[:, columns], load_sem.at[0])
    kept.start()
    copies.wait_send()
    kept.wait()
    handed.wait_recv()
    assert len(copies.started) <= N_COPIES, len(copies.started)


def compute_scratch(channels):
    bf16, f32 = jnp.bfloat16, jnp.float32
    return [
        pltpu.VMEM((4, 16, 16, channels), bf16),
        pltpu.VMEM((3, 2, 8, 16, channels), bf16),
        pltpu.VMEM((CHUNKS * 64, channels), bf16),
        pltpu.VMEM((6, LANES, channels), bf16),
        pltpu.VMEM((CHUNKS * 8 + EDGE, 9, 16, LANES), bf16),
        pltpu.VMEM((2 * PAIRS, 72, LANES), f32),
        pltpu.VMEM((CELLS * HID, COLS), bf16),
        pltpu.VMEM((CELLS * HID, LANES), f32),
        pltpu.VMEM((72, CELLS * HID), bf16),
        pltpu.VMEM((GROUP, CELLS * HID, 256), bf16),
        pltpu.VMEM((2, 2 * HALF, LANES), f32),
        pltpu.VMEM((2, 2 * HALF, LANES), f32),
    ]


def per_device(features_a, features_b, weight_one, bias_one, weight_two, bias_two):
    channels = features_a.shape[-1]
    arguments = (features_a, features_b, weight_one, bias_one, weight_two, bias_two)
    vmem = [pltpu.VMEM(v.shape, v.dtype) for v in (features_a, features_b, weight_one, weight_two)]
    smem = [pltpu.SMEM(v.shape, v.dtype) for v in (bias_one, bias_two)]
    rows = pl.pallas_call(
        kernel,
        out_shape=jax.ShapeDtypeStruct((2, 2 * LANES, LANES), jnp.float32),
        in_specs=[pl.BlockSpec(memory_space=pl.ANY)] * 6,
        out_specs=pl.BlockSpec(memory_space=pl.ANY),
        scratch_shapes=vmem
        + smem
        + [pltpu.SemaphoreType.DMA((6,))]
        + compute_scratch(channels)
        + [pltpu.SemaphoreType.DMA((N_COPIES,)), pltpu.SemaphoreType.DMA((N_COPIES + 4,))],
        compiler_params=pltpu.CompilerParams(
            collective_id=0, has_side_effects=True, vmem_limit_bytes=60 * 1024 * 1024
        ),
        name="consensus",
    )(*arguments)
    return rows.reshape(2, LANES, 2, LANES)


def solution(mesh):
    return jax.shard_map(
        per_device,
        mesh=mesh,
        in_specs=(P("ra", "rb", None), P("rb", "ra", None), P(), P(), P(), P()),
        out_specs=P("ra", None, "rb", None),
        check_vma=False,
    )
```

```python
import jax
import jax.numpy as jnp
from jax import lax
from jax.experimental import pallas as pl
from jax.experimental.pallas import tpu as pltpu
from jax.sharding import PartitionSpec as P

HID = 16
LANES = 128
COLS = 512
USED = 432
CELLS = 24
HALF = 64
CHUNKS = 9


def steps(values, size, count):
    total = jnp.zeros_like(values)
    for n in range(1, count):
        total = total + (values >= n * size).astype(jnp.int32)
    return total


def iota(shape, axis):
    return lax.broadcasted_iota(jnp.int32, shape, axis)


def as_bf16(mask):
    return jnp.where(mask, 1.0, 0.0).astype(jnp.bfloat16)


def normalized(ref):
    values = ref[...].astype(jnp.float32)
    scale = lax.rsqrt(jnp.sum(values * values, axis=-1, keepdims=True) + 1e-06)
    return (values * scale).reshape(16, values.shape[-1]).astype(jnp.bfloat16)


def in_range(index, count):
    return jnp.logical_and(index >= 0, index < count)


class Copies:
    def __init__(self, send_sem, recv_sem):
        self.send_sem, self.recv_sem = send_sem, recv_sem
        self.started, self.waiting = [], []

    def start(self, src, dst, device, arrives=None, later=False):
        n = len(self.started)
        copy = pltpu.make_async_remote_copy(
            src_ref=src,
            dst_ref=dst,
            send_sem=self.send_sem.at[n],
            recv_sem=self.recv_sem.at[n if arrives is None else arrives],
            device_id=device,
            device_id_type=pl.DeviceIdType.MESH,
        )
        if later:
            return copy
        copy.start()
        self.started.append(copy)
        self.waiting.append((copy, None))
        return copy

    def start_when(self, copy, when):
        pl.when(when)(copy.start)
        self.started.append(copy)
        self.waiting.append((copy, when))

    def wait_send(self):
        started, self.waiting = self.waiting, []
        for copy, when in started:
            if when is None:
                copy.wait_send()
            else:
                pl.when(when)(copy.wait_send)


N_COPIES = 100
CHAIN = N_COPIES


class Place:
    def __init__(self, ra, rb):
        self.ra, self.rb = ra, rb
        self.x, self.zh, self.c = lax.div(ra, 4), lax.rem(lax.div(ra, 2), 2), lax.rem(ra, 2)
        self.y, self.zl = lax.div(rb, 4), lax.rem(rb, 4)
        self.chip = lax.div(ra, 2)
        flipped = (self.x * 2 + 1 - self.zh) * 2 + self.c
        self.mate = (ra + 1 - 2 * self.c, rb)
        self.far = (flipped, rb)
        self.line = [(ra, self.y * 4 + lax.rem(self.zl + t, 4)) for t in (1, 2, 3)]
        self.right_y, self.left_y = (ra, lax.rem(rb + 4, 16)), (ra, lax.rem(rb + 12, 16))
        self.right_x, self.left_x = (lax.rem(ra + 4, 16), rb), (lax.rem(ra + 12, 16), rb)
        self.next_b = (jnp.where(self.zl == 3, flipped, ra), lax.rem(rb + 1, 16))
        self.prev_b = (jnp.where(self.zl == 0, flipped, ra), lax.rem(rb + 15, 16))
        self.outer = lax.rem(ra + 2 * self.c + 15, 16)


def greet(p):
    barrier = pltpu.get_barrier_semaphore()

    def signal(device):
        pl.semaphore_signal(barrier, inc=1, device_id=device, device_id_type=pl.DeviceIdType.MESH)

    partners = [p.mate, p.far, p.right_y, p.left_y, p.right_x, p.left_x, p.next_b, p.prev_b]
    for device in partners + p.line:
        signal(device)

    @pl.when(p.zl == 0)
    def _():
        signal((p.outer, p.y * 4 + 2))
        signal((p.outer, p.y * 4 + 3))

    @pl.when(p.zl == 3)
    def _():
        signal((p.outer, p.y * 4))
        signal((p.outer, p.y * 4 + 1))

    return barrier, len(partners) + len(p.line) + 1


def gather(p, a_rows, b_rows, send_sem, recv_sem, meanwhile, have_b):
    copies = Copies(send_sem, recv_sem)
    x, zh, c, y, zl, rb = p.x, p.zh, p.c, p.y, p.zl, p.rb
    so, oo = 1 + c, 3 * c

    def mate_a(slot, index, count=1):
        part = a_rows.at[slot, pl.ds(index, count)]
        return copies.start(part, part, p.mate)

    def mate_b(q, index, count=1):
        part = b_rows.at[q, c, pl.ds(index, count)]
        return copies.start(part, part, p.mate)

    def chunk_a(slot, index):
        return a_rows.at[slot, index]

    def chunk_b(q, index):
        return b_rows.at[q, c, index]

    def to_y(slot, index):
        mates_a.append(mate_a(slot, index))
        return [
            copies.start(chunk_a(slot, index), chunk_a(slot, index), d)
            for d in (p.right_y, p.left_y)
        ]

    def to_x(q, index):
        mates_b.append(mate_b(q, index))
        return [
            copies.start(chunk_b(q, index), chunk_b(q, index), d) for d in (p.right_x, p.left_x)
        ]

    def to_rb(index):
        return [
            copies.start(chunk_b(1, index), chunk_b(0, index), p.next_b),
            copies.start(chunk_b(1, index), chunk_b(2, index), p.prev_b),
        ]

    here, there = x * 2 + zh, x * 2 + 1 - zh
    mates_a, mates_b = [], []

    b_far = copies.start(chunk_b(1, here), chunk_b(1, here), p.far)
    rb_own = to_rb(here)
    end = (p.outer, y * 4 + jnp.where(zl >= 2, 0, 3))
    copies.start(chunk_a(so, rb), chunk_a(3 - oo, rb), end, arrives=CHAIN + zl)
    z_own = [copies.start(chunk_a(so, rb), chunk_a(so, rb), d) for d in p.line]
    y_own = [to_y(so, rb)]
    x_own = [to_x(1, here)]

    meanwhile()

    near = zl < 2
    y_outer = []

    def chain(source):
        column = y * 4 + source
        onward = jnp.where(source >= 2, zl + 1, zl - 1)
        chunk = chunk_a(oo, column)
        neighbour = (p.ra, y * 4 + lax.rem(onward + 4, 4))
        copy = copies.start(chunk, chunk, neighbour, arrives=CHAIN + source, later=True)
        copy.wait_recv()
        copies.start_when(copy, in_range(onward, 4))
        y_outer.append(to_y(oo, column))

    columns = [y * 4 + lax.rem(zl + 4 - t, 4) for t in range(4)]

    def line(t):
        z_own[t - 1].wait_recv()
        y_own.append(to_y(so, columns[t]))

    chain_order = [jnp.where(near, 3, 0), jnp.where(near, 2, 1), jnp.where(near, 0, 3), jnp.where(near, 1, 2)]
    from_prev = [jnp.where(zl == 0, there, here), jnp.where(zl == 0, here, there)]
    from_next = [jnp.where(zl == 3, there, here), jnp.where(zl == 3, here, there)]

    for q, copy, index in ((0, rb_own[0], from_prev[0]), (2, rb_own[1], from_next[0])):
        copy.wait_recv()
        x_own.append(to_x(q, index))
    chain(chain_order[0])
    line(1)
    b_far.wait_recv()
    rb_far = to_rb(there)
    x_far = [to_x(1, there)]
    chain(chain_order[1])
    line(3)
    line(2)

    left_col = [lax.rem(y + 3, 4) * 4 + lax.rem(zl + 4 - t, 4) for t in range(4)]
    order = (0, 1, 3, 2)
    y_on = []

    def own_on(m):
        y_own[m][0].wait_recv()
        chunk = chunk_a(so, left_col[order[m]])
        y_on.append(copies.start(chunk, chunk, p.right_y))

    own_on(0)
    for q, copy, index in ((0, rb_far[0], from_prev[1]), (2, rb_far[1], from_next[1])):
        copy.wait_recv()
        x_far.append(to_x(q, index))
    chain(chain_order[2])
    own_on(1)
    chain(chain_order[3])
    own_on(2)
    own_on(3)

    on_left, on_right = lax.rem(x + 3, 4) * 2, lax.rem(x + 1, 4) * 2
    x_on = []

    def b_on(m):
        q = (1, 0, 2)[m]
        for pair in (x_own[m], x_far[m]):
            for copy in pair:
                copy.wait_recv()
        for index, device in ((on_left, p.right_x), (on_right + 1, p.left_x)):
            x_on.append(copies.start(chunk_b(q, index), chunk_b(q, index), device))
        mates_b.append(mate_b(q, on_left, 2))
        mates_b.append(mate_b(q, on_right, 2))

    outer_on = []

    def a_on(m):
        y_outer[m][1].wait_recv()
        chunk = chunk_a(oo, lax.rem(y + 1, 4) * 4 + chain_order[m])
        outer_on.append(copies.start(chunk, chunk, p.left_y))

    b_on(0)
    a_on(0)
    a_on(1)
    b_on(1)
    b_on(2)
    a_on(2)
    a_on(3)
    for copy in y_own:
        copy[1].wait_recv()
    for copy in y_outer:
        copy[0].wait_recv()
    for slot in (so, oo):
        for side in (3, 1):
            mates_a.append(mate_a(slot, lax.rem(y + side, 4) * 4, 4))
    across = lax.rem(x + 2, 4) * 2
    for n, copy in enumerate(x_on):
        copy.wait_recv()
        if n % 2 == 1:
            mates_b.append(mate_b((1, 0, 2)[n // 2], across, 2))
    for slot, arrivals in ((so, y_on), (oo, outer_on)):
        for copy in arrivals:
            copy.wait_recv()
        mates_a.append(mate_a(slot, lax.rem(y + 2, 4) * 4, 4))
    copies.wait_send()
    for copy in mates_b:
        copy.wait_recv()
    have_b()
    for copy in mates_a:
        copy.wait_recv()
    return copies


def weights(p, w1_ref, bias1_ref, w2_ref, big1, bias_big, big2):
    f32, bf16 = jnp.float32, jnp.bfloat16
    channel = iota((HID, LANES), 0)
    bias = jnp.zeros((HID, LANES), f32)
    for o in range(HID):
        bias = jnp.where(channel == o, bias1_ref[o], bias)
    w1 = w1_ref[...]
    tap = iota((81, COLS), 0)
    col = iota((1, COLS), 1)
    group = steps(col, 48, 11)
    tap_j = steps(group, 3, 4)
    shift = group - 3 * tap_j
    rest = col - 48 * group
    ki = steps(rest, 8, 6)
    ii = rest - 8 * ki
    for io in range(6):
        for ko in range(4):
            n = io * 4 + ko
            inside = jnp.logical_and(in_range(4 * p.chip - 1 + io, 32), in_range(2 * p.rb - 1 + ko, 32))
            inside = inside.astype(f32)
            a, c = ii - io, ki - ko
            fits = jnp.logical_and(jnp.logical_and(a >= 0, a < 3), jnp.logical_and(c >= 0, c < 3))
            wanted = jnp.where(
                jnp.logical_and(fits, col < USED), 27 * a + 9 * tap_j + 3 * c + shift, -1
            )
            block = jnp.dot(w1, as_bf16(tap == wanted), preferred_element_type=f32)
            big1[n * HID : (n + 1) * HID, :] = (block * inside).astype(bf16)
            bias_big[n * HID : (n + 1) * HID, :] = bias * inside
    tile = as_bf16(iota((HID, CELLS * HID), 0) == jnp.bitwise_and(iota((HID, CELLS * HID), 1), HID - 1))
    spread = lax.dot_general(
        w2_ref[...], tile, (((0,), (0,)), ((), ())), preferred_element_type=f32
    ).astype(bf16)
    row = iota((72, 1), 0)
    group = jnp.right_shift(row, 3)
    tap_j = steps(group, 3, 3)
    shift = group - 3 * tap_j
    i = jnp.bitwise_and(jnp.right_shift(row, 1) + 2 * p.c, 3)
    k = jnp.bitwise_and(row, 1)
    cell = jnp.right_shift(iota((72, CELLS * HID), 1), 4)
    tap = iota((72, 81), 1)
    total = jnp.zeros((72, CELLS * HID), f32)
    for a in range(3):
        for c in range(3):
            wanted = 27 * a + 9 * tap_j + 3 * c + shift
            term = jnp.dot(as_bf16(tap == wanted), spread, preferred_element_type=f32)
            total = total + jnp.where(cell == (i + a) * 4 + k + c, term, 0.0)
    big2[...] = total.astype(bf16)


def shifted(values, by):
    lane = lax.broadcasted_iota(jnp.int32, values.shape, values.ndim - 1)
    moved = pltpu.roll(values, (-by) % LANES, values.ndim - 1)
    return jnp.where(lane == (0 if by < 0 else LANES - 1), jnp.zeros_like(moved), moved)


def arrange_a(p, a_rows, a_perm):
    row, col = iota((64, 64), 0), iota((64, 64), 1)
    ii, jj = jnp.bitwise_and(row, 7), jnp.right_shift(row, 3)
    inside = in_range(4 * p.chip - 2 + ii, 32)
    select = as_bf16(jnp.logical_and(inside, col == ii * 8 + jj))
    for n in range(CHUNKS):
        part = jnp.concatenate([a_rows[slot, 7 * p.c + n] for slot in range(4)], axis=0)
        a_perm[n * 64 : (n + 1) * 64, :] = jnp.dot(
            select, part, preferred_element_type=jnp.float32
        ).astype(jnp.bfloat16)


def arrange_b(p, b_rows, b_perm):
    for q in range(3):
        valid = in_range(p.rb - 1 + q, 16)
        for n in range(8):
            both = [b_rows[q, c, n].astype(jnp.float32) for c in range(2)]
            for k in range(2):
                rows16 = jnp.concatenate([v[8 * k : 8 * k + 8] for v in both], axis=0)
                b_perm[2 * q + k, 16 * n : 16 * n + 16, :] = jnp.where(
                    valid, rows16, 0.0
                ).astype(jnp.bfloat16)


J_STEP = 24
EDGE = 8


def correlate(p, a_perm, b_perm, patches):
    f32 = jnp.float32
    patches[pl.ds(CHUNKS * 8 * p.c, EDGE)] = jnp.zeros((EDGE, 9, 16, LANES), jnp.bfloat16)
    base = EDGE * (1 - p.c)
    for n in range(CHUNKS * 8 // J_STEP):
        part = a_perm[n * J_STEP * 8 : (n + 1) * J_STEP * 8, :]
        for pair in range(3):
            both = []
            for k in range(2):
                corr = lax.dot_general(
                    part, b_perm[2 * pair + k], (((1,), (1,)), ((), ())), preferred_element_type=f32
                )
                both.append(corr.reshape(J_STEP, 8, LANES))
            tile = jnp.concatenate(both, axis=1)
            for s in range(3):
                moved = tile if s == 1 else shifted(tile, s - 1)
                patches[pl.ds(base + n * J_STEP, J_STEP), s * 3 + pair] = moved.astype(jnp.bfloat16)


GROUP = 33
PAIRS = 33


def layers(p, patches, big1, bias_big, big2, hidden, taps):
    f32 = jnp.float32

    def one(n, _):
        for u in range(GROUP):
            j = (n * GROUP + u) * 2 + EDGE - 2
            left = patches[pl.ds(j, 3)].reshape(USED, LANES)
            right = patches[pl.ds(j + 1, 3)].reshape(USED, LANES)
            before = jnp.dot(
                big1[:, :USED], jnp.concatenate([left, right], axis=1), preferred_element_type=f32
            )
            bias = bias_big[...]
            hidden[u] = jnp.maximum(before + jnp.concatenate([bias, bias], axis=1), 0.0).astype(
                jnp.bfloat16
            )
        for u in range(GROUP):
            j = (n * GROUP + u) * 2
            out = jnp.dot(big2[...], hidden[u], preferred_element_type=f32)
            taps[j] = out[:, :LANES]
            taps[j + 1] = out[:, LANES:]
        return 0

    lax.fori_loop(0, PAIRS // GROUP, one, 0)
    taps[(2 * PAIRS - 1) * p.c] = jnp.zeros((72, LANES), f32)


def finish(taps, bias2, own, other):
    step = 16
    for n in range(HALF // step):
        start = n * step
        sums = []
        for d in range(3):
            total = None
            for b in range(3):
                row = (b * 3 + d) * 8
                part = taps[start + b : start + b + step, row : row + 8]
                total = part if total is None else total + part
            sums.append(total)
        value = sums[1] + shifted(sums[0], -1) + shifted(sums[2], 1)
        value = jnp.maximum(value + bias2, 0.0)
        for i in range(2):
            rows = slice(2 * start, 2 * (start + step))
            own[i, rows] = value[:, 2 * i : 2 * i + 2].reshape(2 * step, LANES)
            other[i, rows] = value[:, 4 + 2 * i : 6 + 2 * i].reshape(2 * step, LANES)


def kernel(
    a_hbm, b_hbm, w1_hbm, bias1_hbm, w2_hbm, bias2_hbm,
    out_hbm,
    a_ref, b_ref, w1_ref, w2_ref, bias1_ref, bias2_ref, load_sem,
    a_rows, b_rows, a_perm, b_perm, patches, taps, big1, bias_big, big2, hidden, own, other,
    send_sem, recv_sem,
):
    p = Place(lax.axis_index("ra"), lax.axis_index("rb"))
    barrier, count = greet(p)
    pairs = (
        (a_hbm, a_ref), (b_hbm, b_ref), (w1_hbm, w1_ref),
        (w2_hbm, w2_ref), (bias1_hbm, bias1_ref), (bias2_hbm, bias2_ref),
    )
    loads = [
        pltpu.make_async_copy(src, dst, load_sem.at[n]) for n, (src, dst) in enumerate(pairs)
    ]
    for load in loads:
        load.start()
    loads[0].wait()
    a_rows[1 + p.c, p.rb] = normalized(a_ref)
    loads[1].wait()
    b_rows[1, p.c, p.x * 2 + p.zh] = normalized(b_ref)
    pl.semaphore_wait(barrier, count)

    def meanwhile():
        for load in loads[2:]:
            load.wait()
        weights(p, w1_ref, bias1_ref, w2_ref, big1, bias_big, big2)

    def have_b():
        arrange_b(p, b_rows, b_perm)

    copies = gather(p, a_rows, b_rows, send_sem, recv_sem, meanwhile, have_b)
    arrange_a(p, a_rows, a_perm)
    correlate(p, a_perm, b_perm, patches)
    layers(p, patches, big1, bias_big, big2, hidden, taps)
    finish(taps, bias2_ref[0], own, other)
    columns = pl.ds(2 * HALF * p.c, 2 * HALF)
    handed = copies.start(other, out_hbm.at[:, columns], p.mate)
    kept = pltpu.make_async_copy(own, out_hbm.at[:, columns], load_sem.at[0])
    kept.start()
    copies.wait_send()
    kept.wait()
    handed.wait_recv()
    assert len(copies.started) <= N_COPIES, len(copies.started)


def compute_scratch(channels):
    bf16, f32 = jnp.bfloat16, jnp.float32
    return [
        pltpu.VMEM((4, 16, 16, channels), bf16),
        pltpu.VMEM((3, 2, 8, 16, channels), bf16),
        pltpu.VMEM((CHUNKS * 64, channels), bf16),
        pltpu.VMEM((6, LANES, channels), bf16),
        pltpu.VMEM((CHUNKS * 8 + EDGE, 9, 16, LANES), bf16),
        pltpu.VMEM((2 * PAIRS, 72, LANES), f32),
        pltpu.VMEM((CELLS * HID, COLS), bf16),
        pltpu.VMEM((CELLS * HID, LANES), f32),
        pltpu.VMEM((72, CELLS * HID), bf16),
        pltpu.VMEM((GROUP, CELLS * HID, 256), bf16),
        pltpu.VMEM((2, 2 * HALF, LANES), f32),
        pltpu.VMEM((2, 2 * HALF, LANES), f32),
    ]


def per_device(features_a, features_b, weight_one, bias_one, weight_two, bias_two):
    channels = features_a.shape[-1]
    arguments = (features_a, features_b, weight_one, bias_one, weight_two, bias_two)
    vmem = [pltpu.VMEM(v.shape, v.dtype) for v in (features_a, features_b, weight_one, weight_two)]
    smem = [pltpu.SMEM(v.shape, v.dtype) for v in (bias_one, bias_two)]
    rows = pl.pallas_call(
        kernel,
        out_shape=jax.ShapeDtypeStruct((2, 2 * LANES, LANES), jnp.float32),
        in_specs=[pl.BlockSpec(memory_space=pl.ANY)] * 6,
        out_specs=pl.BlockSpec(memory_space=pl.ANY),
        scratch_shapes=vmem
        + smem
        + [pltpu.SemaphoreType.DMA((6,))]
        + compute_scratch(channels)
        + [pltpu.SemaphoreType.DMA((N_COPIES,)), pltpu.SemaphoreType.DMA((N_COPIES + 4,))],
        compiler_params=pltpu.CompilerParams(
            collective_id=0, has_side_effects=True, vmem_limit_bytes=60 * 1024 * 1024
        ),
        name="consensus",
    )(*arguments)
    return rows.reshape(2, LANES, 2, LANES)


def solution(mesh):
    return jax.shard_map(
        per_device,
        mesh=mesh,
        in_specs=(P("ra", "rb", None), P("rb", "ra", None), P(), P(), P(), P()),
        out_specs=P("ra", None, "rb", None),
        check_vma=False,
    )
```

```python
import jax
import jax.numpy as jnp
from jax import lax
from jax.experimental import pallas as pl
from jax.experimental.pallas import tpu as pltpu
from jax.sharding import PartitionSpec as P

HID = 16
LANES = 128
COLS = 512
USED = 432
CELLS = 24
HALF = 64
CHUNKS = 9


def steps(values, size, count):
    total = jnp.zeros_like(values)
    for n in range(1, count):
        total = total + (values >= n * size).astype(jnp.int32)
    return total


def iota(shape, axis):
    return lax.broadcasted_iota(jnp.int32, shape, axis)


def as_bf16(mask):
    return jnp.where(mask, 1.0, 0.0).astype(jnp.bfloat16)


def normalized(ref):
    values = ref[...].astype(jnp.float32)
    scale = lax.rsqrt(jnp.sum(values * values, axis=-1, keepdims=True) + 1e-06)
    return (values * scale).reshape(16, values.shape[-1]).astype(jnp.bfloat16)


def in_range(index, count):
    return jnp.logical_and(index >= 0, index < count)


class Copies:
    def __init__(self, send_sem, recv_sem):
        self.send_sem, self.recv_sem = send_sem, recv_sem
        self.started, self.waiting = [], []

    def start(self, src, dst, device, arrives=None, later=False):
        n = len(self.started)
        copy = pltpu.make_async_remote_copy(
            src_ref=src,
            dst_ref=dst,
            send_sem=self.send_sem.at[n],
            recv_sem=self.recv_sem.at[n if arrives is None else arrives],
            device_id=device,
            device_id_type=pl.DeviceIdType.MESH,
        )
        if later:
            return copy
        copy.start()
        self.started.append(copy)
        self.waiting.append((copy, None))
        return copy

    def start_when(self, copy, when):
        pl.when(when)(copy.start)
        self.started.append(copy)
        self.waiting.append((copy, when))

    def wait_send(self):
        started, self.waiting = self.waiting, []
        for copy, when in started:
            if when is None:
                copy.wait_send()
            else:
                pl.when(when)(copy.wait_send)


N_COPIES = 100
CHAIN = N_COPIES


class Place:
    def __init__(self, ra, rb):
        self.ra, self.rb = ra, rb
        self.x, self.zh, self.c = lax.div(ra, 4), lax.rem(lax.div(ra, 2), 2), lax.rem(ra, 2)
        self.y, self.zl = lax.div(rb, 4), lax.rem(rb, 4)
        self.chip = lax.div(ra, 2)
        flipped = (self.x * 2 + 1 - self.zh) * 2 + self.c
        self.mate = (ra + 1 - 2 * self.c, rb)
        self.far = (flipped, rb)
        self.line = [(ra, self.y * 4 + lax.rem(self.zl + t, 4)) for t in (1, 2, 3)]
        self.right_y, self.left_y = (ra, lax.rem(rb + 4, 16)), (ra, lax.rem(rb + 12, 16))
        self.right_x, self.left_x = (lax.rem(ra + 4, 16), rb), (lax.rem(ra + 12, 16), rb)
        self.next_b = (jnp.where(self.zl == 3, flipped, ra), lax.rem(rb + 1, 16))
        self.prev_b = (jnp.where(self.zl == 0, flipped, ra), lax.rem(rb + 15, 16))
        self.outer = lax.rem(ra + 2 * self.c + 15, 16)


def greet(p):
    barrier = pltpu.get_barrier_semaphore()

    def signal(device):
        pl.semaphore_signal(barrier, inc=1, device_id=device, device_id_type=pl.DeviceIdType.MESH)

    partners = [p.mate, p.far, p.right_y, p.left_y, p.right_x, p.left_x, p.next_b, p.prev_b]
    for device in partners + p.line:
        signal(device)

    @pl.when(p.zl == 0)
    def _():
        signal((p.outer, p.y * 4 + 2))
        signal((p.outer, p.y * 4 + 3))

    @pl.when(p.zl == 3)
    def _():
        signal((p.outer, p.y * 4))
        signal((p.outer, p.y * 4 + 1))

    return barrier, len(partners) + len(p.line) + 1


def gather(p, a_rows, b_rows, send_sem, recv_sem, meanwhile, have_b):
    copies = Copies(send_sem, recv_sem)
    x, zh, c, y, zl, rb = p.x, p.zh, p.c, p.y, p.zl, p.rb
    so, oo = 1 + c, 3 * c

    def mate_a(slot, index, count=1):
        part = a_rows.at[slot, pl.ds(index, count)]
        return copies.start(part, part, p.mate)

    def mate_b(q, index, count=1):
        part = b_rows.at[q, c, pl.ds(index, count)]
        return copies.start(part, part, p.mate)

    def chunk_a(slot, index):
        return a_rows.at[slot, index]

    def chunk_b(q, index):
        return b_rows.at[q, c, index]

    def to_y(slot, index):
        mates_a.append(mate_a(slot, index))
        return [
            copies.start(chunk_a(slot, index), chunk_a(slot, index), d)
            for d in (p.right_y, p.left_y)
        ]

    def to_x(q, index):
        mates_b.append(mate_b(q, index))
        return [
            copies.start(chunk_b(q, index), chunk_b(q, index), d) for d in (p.right_x, p.left_x)
        ]

    def to_rb(index):
        return [
            copies.start(chunk_b(1, index), chunk_b(0, index), p.next_b),
            copies.start(chunk_b(1, index), chunk_b(2, index), p.prev_b),
        ]

    here, there = x * 2 + zh, x * 2 + 1 - zh
    mates_a, mates_b = [], []

    b_far = copies.start(chunk_b(1, here), chunk_b(1, here), p.far)
    rb_own = to_rb(here)
    end = (p.outer, y * 4 + jnp.where(zl >= 2, 0, 3))
    copies.start(chunk_a(so, rb), chunk_a(3 - oo, rb), end, arrives=CHAIN + zl)
    z_own = [copies.start(chunk_a(so, rb), chunk_a(so, rb), d) for d in p.line]
    y_own = [to_y(so, rb)]
    x_own = [to_x(1, here)]

    meanwhile()

    near = zl < 2
    y_outer = []

    def chain(source):
        column = y * 4 + source
        onward = jnp.where(source >= 2, zl + 1, zl - 1)
        chunk = chunk_a(oo, column)
        neighbour = (p.ra, y * 4 + lax.rem(onward + 4, 4))
        copy = copies.start(chunk, chunk, neighbour, arrives=CHAIN + source, later=True)
        copy.wait_recv()
        copies.start_when(copy, in_range(onward, 4))
        y_outer.append(to_y(oo, column))

    columns = [y * 4 + lax.rem(zl + 4 - t, 4) for t in range(4)]

    def line(t):
        z_own[t - 1].wait_recv()
        y_own.append(to_y(so, columns[t]))

    chain_order = [jnp.where(near, 3, 0), jnp.where(near, 2, 1), jnp.where(near, 0, 3), jnp.where(near, 1, 2)]
    from_prev = [jnp.where(zl == 0, there, here), jnp.where(zl == 0, here, there)]
    from_next = [jnp.where(zl == 3, there, here), jnp.where(zl == 3, here, there)]

    for q, copy, index in ((0, rb_own[0], from_prev[0]), (2, rb_own[1], from_next[0])):
        copy.wait_recv()
        x_own.append(to_x(q, index))
    chain(chain_order[0])
    line(1)
    b_far.wait_recv()
    rb_far = to_rb(there)
    x_far = [to_x(1, there)]
    chain(chain_order[1])
    line(3)
    line(2)

    left_col = [lax.rem(y + 3, 4) * 4 + lax.rem(zl + 4 - t, 4) for t in range(4)]
    order = (0, 1, 3, 2)
    y_on = []

    def own_on(m):
        y_own[m][0].wait_recv()
        chunk = chunk_a(so, left_col[order[m]])
        y_on.append(copies.start(chunk, chunk, p.right_y))

    own_on(0)
    for q, copy, index in ((0, rb_far[0], from_prev[1]), (2, rb_far[1], from_next[1])):
        copy.wait_recv()
        x_far.append(to_x(q, index))
    chain(chain_order[2])
    own_on(1)
    chain(chain_order[3])
    own_on(2)
    own_on(3)

    on_left, on_right = lax.rem(x + 3, 4) * 2, lax.rem(x + 1, 4) * 2
    x_on = []

    def b_on(m):
        q = (1, 0, 2)[m]
        for pair in (x_own[m], x_far[m]):
            for copy in pair:
                copy.wait_recv()
        for index, device in ((on_left, p.right_x), (on_right + 1, p.left_x)):
            x_on.append(copies.start(chunk_b(q, index), chunk_b(q, index), device))
        mates_b.append(mate_b(q, on_left, 2))
        mates_b.append(mate_b(q, on_right, 2))

    outer_on = []

    def a_on(m):
        y_outer[m][1].wait_recv()
        chunk = chunk_a(oo, lax.rem(y + 1, 4) * 4 + chain_order[m])
        outer_on.append(copies.start(chunk, chunk, p.left_y))

    b_on(0)
    a_on(0)
    a_on(1)
    b_on(1)
    b_on(2)
    a_on(2)
    a_on(3)
    for copy in y_own:
        copy[1].wait_recv()
    for copy in y_outer:
        copy[0].wait_recv()
    for slot in (so, oo):
        for side in (3, 1):
            mates_a.append(mate_a(slot, lax.rem(y + side, 4) * 4, 4))
    across = lax.rem(x + 2, 4) * 2
    for n, copy in enumerate(x_on):
        copy.wait_recv()
        if n % 2 == 1:
            mates_b.append(mate_b((1, 0, 2)[n // 2], across, 2))
    for slot, arrivals in ((so, y_on), (oo, outer_on)):
        for copy in arrivals:
            copy.wait_recv()
        mates_a.append(mate_a(slot, lax.rem(y + 2, 4) * 4, 4))
    copies.wait_send()
    for copy in mates_b:
        copy.wait_recv()
    have_b()
    for copy in mates_a:
        copy.wait_recv()
    return copies


def weights(p, w1_ref, bias1_ref, w2_ref, big1, bias_big, big2):
    f32, bf16 = jnp.float32, jnp.bfloat16
    channel = iota((HID, LANES), 0)
    bias = jnp.zeros((HID, LANES), f32)
    for o in range(HID):
        bias = jnp.where(channel == o, bias1_ref[o], bias)
    w1 = w1_ref[...]
    tap = iota((81, COLS), 0)
    col = iota((1, COLS), 1)
    group = steps(col, 48, 11)
    tap_j = steps(group, 3, 4)
    shift = group - 3 * tap_j
    rest = col - 48 * group
    ki = steps(rest, 8, 6)
    ii = rest - 8 * ki
    for io in range(6):
        for ko in range(4):
            n = io * 4 + ko
            inside = jnp.logical_and(in_range(4 * p.chip - 1 + io, 32), in_range(2 * p.rb - 1 + ko, 32))
            inside = inside.astype(f32)
            a, c = ii - io, ki - ko
            fits = jnp.logical_and(jnp.logical_and(a >= 0, a < 3), jnp.logical_and(c >= 0, c < 3))
            wanted = jnp.where(
                jnp.logical_and(fits, col < USED), 27 * a + 9 * tap_j + 3 * c + shift, -1
            )
            block = jnp.dot(w1, as_bf16(tap == wanted), preferred_element_type=f32)
            big1[n * HID : (n + 1) * HID, :] = (block * inside).astype(bf16)
            bias_big[n * HID : (n + 1) * HID, :] = bias * inside
    tile = as_bf16(iota((HID, CELLS * HID), 0) == jnp.bitwise_and(iota((HID, CELLS * HID), 1), HID - 1))
    spread = lax.dot_general(
        w2_ref[...], tile, (((0,), (0,)), ((), ())), preferred_element_type=f32
    ).astype(bf16)
    row = iota((72, 1), 0)
    group = jnp.right_shift(row, 3)
    tap_j = steps(group, 3, 3)
    shift = group - 3 * tap_j
    i = jnp.bitwise_and(jnp.right_shift(row, 1) + 2 * p.c, 3)
    k = jnp.bitwise_and(row, 1)
    cell = jnp.right_shift(iota((72, CELLS * HID), 1), 4)
    tap = iota((72, 81), 1)
    total = jnp.zeros((72, CELLS * HID), f32)
    for a in range(3):
        for c in range(3):
            wanted = 27 * a + 9 * tap_j + 3 * c + shift
            term = jnp.dot(as_bf16(tap == wanted), spread, preferred_element_type=f32)
            total = total + jnp.where(cell == (i + a) * 4 + k + c, term, 0.0)
    big2[...] = total.astype(bf16)


def shifted(values, by):
    lane = lax.broadcasted_iota(jnp.int32, values.shape, values.ndim - 1)
    moved = pltpu.roll(values, (-by) % LANES, values.ndim - 1)
    return jnp.where(lane == (0 if by < 0 else LANES - 1), jnp.zeros_like(moved), moved)


def arrange_a(p, a_rows, a_perm):
    row, col = iota((64, 64), 0), iota((64, 64), 1)
    ii, jj = jnp.bitwise_and(row, 7), jnp.right_shift(row, 3)
    inside = in_range(4 * p.chip - 2 + ii, 32)
    select = as_bf16(jnp.logical_and(inside, col == ii * 8 + jj))
    for n in range(CHUNKS):
        part = jnp.concatenate([a_rows[slot, 7 * p.c + n] for slot in range(4)], axis=0)
        a_perm[n * 64 : (n + 1) * 64, :] = jnp.dot(
            select, part, preferred_element_type=jnp.float32
        ).astype(jnp.bfloat16)


def arrange_b(p, b_rows, b_perm):
    for q in range(3):
        valid = in_range(p.rb - 1 + q, 16)
        for n in range(8):
            both = [b_rows[q, c, n].astype(jnp.float32) for c in range(2)]
            for k in range(2):
                rows16 = jnp.concatenate([v[8 * k : 8 * k + 8] for v in both], axis=0)
                b_perm[2 * q + k, 16 * n : 16 * n + 16, :] = jnp.where(
                    valid, rows16, 0.0
                ).astype(jnp.bfloat16)


J_STEP = 24
EDGE = 8


def correlate(p, a_perm, b_perm, patches):
    f32 = jnp.float32
    patches[pl.ds(CHUNKS * 8 * p.c, EDGE)] = jnp.zeros((EDGE, 9, 16, LANES), jnp.bfloat16)
    base = EDGE * (1 - p.c)
    for n in range(CHUNKS * 8 // J_STEP):
        part = a_perm[n * J_STEP * 8 : (n + 1) * J_STEP * 8, :]
        for pair in range(3):
            both = []
            for k in range(2):
                corr = lax.dot_general(
                    part, b_perm[2 * pair + k], (((1,), (1,)), ((), ())), preferred_element_type=f32
                )
                both.append(corr.reshape(J_STEP, 8, LANES))
            tile = jnp.concatenate(both, axis=1)
            for s in range(3):
                moved = tile if s == 1 else shifted(tile, s - 1)
                patches[pl.ds(base + n * J_STEP, J_STEP), s * 3 + pair] = moved.astype(jnp.bfloat16)


GROUP = 33
PAIRS = 33


def layers(p, patches, big1, bias_big, big2, hidden, taps):
    f32 = jnp.float32

    def one(n, _):
        for u in range(GROUP):
            j = (n * GROUP + u) * 2 + EDGE - 2
            left = patches[pl.ds(j, 3)].reshape(USED, LANES)
            right = patches[pl.ds(j + 1, 3)].reshape(USED, LANES)
            before = jnp.dot(
                big1[:, :USED], jnp.concatenate([left, right], axis=1), preferred_element_type=f32
            )
            bias = bias_big[...]
            hidden[u] = jnp.maximum(before + jnp.concatenate([bias, bias], axis=1), 0.0).astype(
                jnp.bfloat16
            )
        for u in range(GROUP):
            j = (n * GROUP + u) * 2
            out = jnp.dot(big2[...], hidden[u], preferred_element_type=f32)
            taps[j] = out[:, :LANES]
            taps[j + 1] = out[:, LANES:]
        return 0

    lax.fori_loop(0, PAIRS // GROUP, one, 0)
    taps[(2 * PAIRS - 1) * p.c] = jnp.zeros((72, LANES), f32)


def finish(taps, own, other):
    step = 16
    for n in range(HALF // step):
        start = n * step
        sums = []
        for d in range(3):
            total = None
            for b in range(3):
                row = (b * 3 + d) * 8
                part = taps[start + b : start + b + step, row : row + 8]
                total = part if total is None else total + part
            sums.append(total)
        value = sums[1] + shifted(sums[0], -1) + shifted(sums[2], 1)
        for i in range(2):
            rows = slice(2 * start, 2 * (start + step))
            own[i, rows] = value[:, 2 * i : 2 * i + 2].reshape(2 * step, LANES)
            other[i, rows] = value[:, 4 + 2 * i : 6 + 2 * i].reshape(2 * step, LANES)


def kernel(
    a_hbm, b_hbm, w1_hbm, bias1_hbm, w2_hbm,
    out_hbm,
    a_ref, b_ref, w1_ref, w2_ref, bias1_ref, load_sem,
    a_rows, b_rows, a_perm, b_perm, patches, taps, big1, bias_big, big2, hidden, own, other,
    send_sem, recv_sem,
):
    p = Place(lax.axis_index("ra"), lax.axis_index("rb"))
    barrier, count = greet(p)
    pairs = (
        (a_hbm, a_ref), (b_hbm, b_ref), (w1_hbm, w1_ref),
        (w2_hbm, w2_ref), (bias1_hbm, bias1_ref),
    )
    loads = [
        pltpu.make_async_copy(src, dst, load_sem.at[n]) for n, (src, dst) in enumerate(pairs)
    ]
    for load in loads:
        load.start()
    loads[0].wait()
    a_rows[1 + p.c, p.rb] = normalized(a_ref)
    loads[1].wait()
    b_rows[1, p.c, p.x * 2 + p.zh] = normalized(b_ref)
    pl.semaphore_wait(barrier, count)

    def meanwhile():
        for load in loads[2:]:
            load.wait()
        weights(p, w1_ref, bias1_ref, w2_ref, big1, bias_big, big2)

    def have_b():
        arrange_b(p, b_rows, b_perm)

    copies = gather(p, a_rows, b_rows, send_sem, recv_sem, meanwhile, have_b)
    arrange_a(p, a_rows, a_perm)
    correlate(p, a_perm, b_perm, patches)
    layers(p, patches, big1, bias_big, big2, hidden, taps)
    finish(taps, own, other)
    columns = pl.ds(2 * HALF * p.c, 2 * HALF)
    handed = copies.start(other, out_hbm.at[:, columns], p.mate)
    kept = pltpu.make_async_copy(own, out_hbm.at[:, columns], load_sem.at[0])
    kept.start()
    copies.wait_send()
    kept.wait()
    handed.wait_recv()
    assert len(copies.started) <= N_COPIES, len(copies.started)


def compute_scratch(channels):
    bf16, f32 = jnp.bfloat16, jnp.float32
    return [
        pltpu.VMEM((4, 16, 16, channels), bf16),
        pltpu.VMEM((3, 2, 8, 16, channels), bf16),
        pltpu.VMEM((CHUNKS * 64, channels), bf16),
        pltpu.VMEM((6, LANES, channels), bf16),
        pltpu.VMEM((CHUNKS * 8 + EDGE, 9, 16, LANES), bf16),
        pltpu.VMEM((2 * PAIRS, 72, LANES), f32),
        pltpu.VMEM((CELLS * HID, COLS), bf16),
        pltpu.VMEM((CELLS * HID, LANES), f32),
        pltpu.VMEM((72, CELLS * HID), bf16),
        pltpu.VMEM((GROUP, CELLS * HID, 256), bf16),
        pltpu.VMEM((2, 2 * HALF, LANES), f32),
        pltpu.VMEM((2, 2 * HALF, LANES), f32),
    ]


def per_device(features_a, features_b, weight_one, bias_one, weight_two, bias_two):
    channels = features_a.shape[-1]
    arguments = (features_a, features_b, weight_one, bias_one, weight_two)
    vmem = [pltpu.VMEM(v.shape, v.dtype) for v in (features_a, features_b, weight_one, weight_two)]
    smem = [pltpu.SMEM(v.shape, v.dtype) for v in (bias_one,)]
    rows = pl.pallas_call(
        kernel,
        out_shape=jax.ShapeDtypeStruct((2, 2 * LANES, LANES), jnp.float32),
        in_specs=[pl.BlockSpec(memory_space=pl.ANY)] * 5,
        out_specs=pl.BlockSpec(memory_space=pl.ANY),
        scratch_shapes=vmem
        + smem
        + [pltpu.SemaphoreType.DMA((5,))]
        + compute_scratch(channels)
        + [pltpu.SemaphoreType.DMA((N_COPIES,)), pltpu.SemaphoreType.DMA((N_COPIES + 4,))],
        compiler_params=pltpu.CompilerParams(
            collective_id=0, has_side_effects=True, vmem_limit_bytes=40 * 1024 * 1024
        ),
        name="consensus",
    )(*[pltpu.with_memory_space_constraint(v, pltpu.HBM) for v in arguments])
    return jax.nn.relu(rows.reshape(2, LANES, 2, LANES) + bias_two[0])


def solution(mesh):
    return jax.shard_map(
        per_device,
        mesh=mesh,
        in_specs=(P("ra", "rb", None), P("rb", "ra", None), P(), P(), P(), P()),
        out_specs=P("ra", None, "rb", None),
        check_vma=False,
    )
```

```python
import jax
import jax.numpy as jnp
from jax import lax
from jax.experimental import pallas as pl
from jax.experimental.pallas import tpu as pltpu
from jax.sharding import PartitionSpec as P

HID = 16
LANES = 128
COLS = 512
USED = 432
CELLS = 24
HALF = 64
CHUNKS = 9


def steps(values, size, count):
    total = jnp.zeros_like(values)
    for n in range(1, count):
        total = total + (values >= n * size).astype(jnp.int32)
    return total


def iota(shape, axis):
    return lax.broadcasted_iota(jnp.int32, shape, axis)


def as_bf16(mask):
    return jnp.where(mask, 1.0, 0.0).astype(jnp.bfloat16)


def normalized(ref):
    values = ref[...].astype(jnp.float32)
    scale = lax.rsqrt(jnp.sum(values * values, axis=-1, keepdims=True) + 1e-06)
    return (values * scale).reshape(16, values.shape[-1]).astype(jnp.bfloat16)


def in_range(index, count):
    return jnp.logical_and(index >= 0, index < count)


class Copies:
    def __init__(self, send_sem, recv_sem):
        self.send_sem, self.recv_sem = send_sem, recv_sem
        self.started, self.waiting = [], []

    def start(self, src, dst, device, arrives=None, later=False):
        n = len(self.started)
        copy = pltpu.make_async_remote_copy(
            src_ref=src,
            dst_ref=dst,
            send_sem=self.send_sem.at[n],
            recv_sem=self.recv_sem.at[n if arrives is None else arrives],
            device_id=device,
            device_id_type=pl.DeviceIdType.MESH,
        )
        if later:
            return copy
        copy.start()
        self.started.append(copy)
        self.waiting.append((copy, None))
        return copy

    def start_when(self, copy, when):
        pl.when(when)(copy.start)
        self.started.append(copy)
        self.waiting.append((copy, when))

    def wait_send(self):
        started, self.waiting = self.waiting, []
        for copy, when in started:
            if when is None:
                copy.wait_send()
            else:
                pl.when(when)(copy.wait_send)


N_COPIES = 100
CHAIN = N_COPIES


class Place:
    def __init__(self, ra, rb):
        self.ra, self.rb = ra, rb
        self.x, self.zh, self.c = lax.div(ra, 4), lax.rem(lax.div(ra, 2), 2), lax.rem(ra, 2)
        self.y, self.zl = lax.div(rb, 4), lax.rem(rb, 4)
        self.chip = lax.div(ra, 2)
        flipped = (self.x * 2 + 1 - self.zh) * 2 + self.c
        self.mate = (ra + 1 - 2 * self.c, rb)
        self.far = (flipped, rb)
        self.line = [(ra, self.y * 4 + lax.rem(self.zl + t, 4)) for t in (1, 2, 3)]
        self.right_y, self.left_y = (ra, lax.rem(rb + 4, 16)), (ra, lax.rem(rb + 12, 16))
        self.right_x, self.left_x = (lax.rem(ra + 4, 16), rb), (lax.rem(ra + 12, 16), rb)
        self.next_b = (jnp.where(self.zl == 3, flipped, ra), lax.rem(rb + 1, 16))
        self.prev_b = (jnp.where(self.zl == 0, flipped, ra), lax.rem(rb + 15, 16))
        self.outer = lax.rem(ra + 2 * self.c + 15, 16)


def greet(p):
    barrier = pltpu.get_barrier_semaphore()

    def signal(device):
        pl.semaphore_signal(barrier, inc=1, device_id=device, device_id_type=pl.DeviceIdType.MESH)

    partners = [p.mate, p.far, p.right_y, p.left_y, p.right_x, p.left_x, p.next_b, p.prev_b]
    for device in partners + p.line:
        signal(device)

    @pl.when(p.zl == 0)
    def _():
        signal((p.outer, p.y * 4 + 2))
        signal((p.outer, p.y * 4 + 3))

    @pl.when(p.zl == 3)
    def _():
        signal((p.outer, p.y * 4))
        signal((p.outer, p.y * 4 + 1))

    return barrier, len(partners) + len(p.line) + 1


def gather(p, a_rows, b_rows, send_sem, recv_sem, meanwhile, have_b):
    copies = Copies(send_sem, recv_sem)
    x, zh, c, y, zl, rb = p.x, p.zh, p.c, p.y, p.zl, p.rb
    so, oo = 1 + c, 3 * c

    def mate_a(slot, index, count=1):
        part = a_rows.at[slot, pl.ds(index, count)]
        return copies.start(part, part, p.mate)

    def mate_b(q, index, count=1):
        part = b_rows.at[q, c, pl.ds(index, count)]
        return copies.start(part, part, p.mate)

    def chunk_a(slot, index):
        return a_rows.at[slot, index]

    def chunk_b(q, index):
        return b_rows.at[q, c, index]

    def to_y(slot, index):
        mates_a.append(mate_a(slot, index))
        return [
            copies.start(chunk_a(slot, index), chunk_a(slot, index), d)
            for d in (p.right_y, p.left_y)
        ]

    def to_x(q, index):
        mates_b.append(mate_b(q, index))
        return [
            copies.start(chunk_b(q, index), chunk_b(q, index), d) for d in (p.right_x, p.left_x)
        ]

    def to_rb(index):
        return [
            copies.start(chunk_b(1, index), chunk_b(0, index), p.next_b),
            copies.start(chunk_b(1, index), chunk_b(2, index), p.prev_b),
        ]

    here, there = x * 2 + zh, x * 2 + 1 - zh
    mates_a, mates_b = [], []

    b_far = copies.start(chunk_b(1, here), chunk_b(1, here), p.far)
    rb_own = to_rb(here)
    end = (p.outer, y * 4 + jnp.where(zl >= 2, 0, 3))
    copies.start(chunk_a(so, rb), chunk_a(3 - oo, rb), end, arrives=CHAIN + zl)
    z_own = [copies.start(chunk_a(so, rb), chunk_a(so, rb), d) for d in p.line]
    y_own = [to_y(so, rb)]
    x_own = [to_x(1, here)]

    meanwhile()

    near = zl < 2
    y_outer = []

    def chain(source):
        column = y * 4 + source
        onward = jnp.where(source >= 2, zl + 1, zl - 1)
        chunk = chunk_a(oo, column)
        neighbour = (p.ra, y * 4 + lax.rem(onward + 4, 4))
        copy = copies.start(chunk, chunk, neighbour, arrives=CHAIN + source, later=True)
        copy.wait_recv()
        copies.start_when(copy, in_range(onward, 4))
        y_outer.append(to_y(oo, column))

    columns = [y * 4 + lax.rem(zl + 4 - t, 4) for t in range(4)]

    def line(t):
        z_own[t - 1].wait_recv()
        y_own.append(to_y(so, columns[t]))

    chain_order = [jnp.where(near, 3, 0), jnp.where(near, 2, 1), jnp.where(near, 0, 3), jnp.where(near, 1, 2)]
    from_prev = [jnp.where(zl == 0, there, here), jnp.where(zl == 0, here, there)]
    from_next = [jnp.where(zl == 3, there, here), jnp.where(zl == 3, here, there)]

    for q, copy, index in ((0, rb_own[0], from_prev[0]), (2, rb_own[1], from_next[0])):
        copy.wait_recv()
        x_own.append(to_x(q, index))
    chain(chain_order[0])
    line(1)
    b_far.wait_recv()
    rb_far = to_rb(there)
    x_far = [to_x(1, there)]
    chain(chain_order[1])
    line(3)
    line(2)

    left_col = [lax.rem(y + 3, 4) * 4 + lax.rem(zl + 4 - t, 4) for t in range(4)]
    order = (0, 1, 3, 2)
    y_on = []

    def own_on(m):
        y_own[m][0].wait_recv()
        chunk = chunk_a(so, left_col[order[m]])
        y_on.append(copies.start(chunk, chunk, p.right_y))

    own_on(0)
    for q, copy, index in ((0, rb_far[0], from_prev[1]), (2, rb_far[1], from_next[1])):
        copy.wait_recv()
        x_far.append(to_x(q, index))
    chain(chain_order[2])
    own_on(1)
    chain(chain_order[3])
    own_on(2)
    own_on(3)

    on_left, on_right = lax.rem(x + 3, 4) * 2, lax.rem(x + 1, 4) * 2
    x_on = []

    def b_on(m):
        q = (1, 0, 2)[m]
        for pair in (x_own[m], x_far[m]):
            for copy in pair:
                copy.wait_recv()
        for index, device in ((on_left, p.right_x), (on_right + 1, p.left_x)):
            x_on.append(copies.start(chunk_b(q, index), chunk_b(q, index), device))
        mates_b.append(mate_b(q, on_left, 2))
        mates_b.append(mate_b(q, on_right, 2))

    outer_on = []

    def a_on(m):
        y_outer[m][1].wait_recv()
        chunk = chunk_a(oo, lax.rem(y + 1, 4) * 4 + chain_order[m])
        outer_on.append(copies.start(chunk, chunk, p.left_y))

    b_on(0)
    a_on(0)
    a_on(1)
    b_on(1)
    b_on(2)
    a_on(2)
    a_on(3)
    for copy in y_own:
        copy[1].wait_recv()
    for copy in y_outer:
        copy[0].wait_recv()
    for slot in (so, oo):
        for side in (3, 1):
            mates_a.append(mate_a(slot, lax.rem(y + side, 4) * 4, 4))
    across = lax.rem(x + 2, 4) * 2
    for n, copy in enumerate(x_on):
        copy.wait_recv()
        if n % 2 == 1:
            mates_b.append(mate_b((1, 0, 2)[n // 2], across, 2))
    copies.wait_send()
    for slot, arrivals in ((so, y_on), (oo, outer_on)):
        for copy in arrivals:
            copy.wait_recv()
        mates_a.append(mate_a(slot, lax.rem(y + 2, 4) * 4, 4))
    for copy in mates_b:
        copy.wait_recv()
    have_b()
    for copy in mates_a:
        copy.wait_recv()
    return copies


def weights(p, w1_ref, bias1_ref, w2_ref, big1, bias_big, big2):
    f32, bf16 = jnp.float32, jnp.bfloat16
    channel = iota((HID, LANES), 0)
    bias = jnp.zeros((HID, LANES), f32)
    for o in range(HID):
        bias = jnp.where(channel == o, bias1_ref[o], bias)
    w1 = w1_ref[...]
    tap = iota((81, COLS), 0)
    col = iota((1, COLS), 1)
    group = steps(col, 48, 11)
    tap_j = steps(group, 3, 4)
    shift = group - 3 * tap_j
    rest = col - 48 * group
    ki = steps(rest, 8, 6)
    ii = rest - 8 * ki
    for io in range(6):
        for ko in range(4):
            n = io * 4 + ko
            inside = jnp.logical_and(in_range(4 * p.chip - 1 + io, 32), in_range(2 * p.rb - 1 + ko, 32))
            inside = inside.astype(f32)
            a, c = ii - io, ki - ko
            fits = jnp.logical_and(jnp.logical_and(a >= 0, a < 3), jnp.logical_and(c >= 0, c < 3))
            wanted = jnp.where(
                jnp.logical_and(fits, col < USED), 27 * a + 9 * tap_j + 3 * c + shift, -1
            )
            block = jnp.dot(w1, as_bf16(tap == wanted), preferred_element_type=f32)
            big1[n * HID : (n + 1) * HID, :] = (block * inside).astype(bf16)
            bias_big[n * HID : (n + 1) * HID, :] = bias * inside
    tile = as_bf16(iota((HID, CELLS * HID), 0) == jnp.bitwise_and(iota((HID, CELLS * HID), 1), HID - 1))
    spread = lax.dot_general(
        w2_ref[...], tile, (((0,), (0,)), ((), ())), preferred_element_type=f32
    ).astype(bf16)
    row = iota((72, 1), 0)
    group = jnp.right_shift(row, 3)
    tap_j = steps(group, 3, 3)
    shift = group - 3 * tap_j
    i = jnp.bitwise_and(jnp.right_shift(row, 1) + 2 * p.c, 3)
    k = jnp.bitwise_and(row, 1)
    cell = jnp.right_shift(iota((72, CELLS * HID), 1), 4)
    tap = iota((72, 81), 1)
    total = jnp.zeros((72, CELLS * HID), f32)
    for a in range(3):
        for c in range(3):
            wanted = 27 * a + 9 * tap_j + 3 * c + shift
            term = jnp.dot(as_bf16(tap == wanted), spread, preferred_element_type=f32)
            total = total + jnp.where(cell == (i + a) * 4 + k + c, term, 0.0)
    big2[...] = total.astype(bf16)


def shifted(values, by):
    lane = lax.broadcasted_iota(jnp.int32, values.shape, values.ndim - 1)
    moved = pltpu.roll(values, (-by) % LANES, values.ndim - 1)
    return jnp.where(lane == (0 if by < 0 else LANES - 1), jnp.zeros_like(moved), moved)


def arrange_a(p, a_rows, a_perm):
    row, col = iota((64, 64), 0), iota((64, 64), 1)
    ii, jj = jnp.bitwise_and(row, 7), jnp.right_shift(row, 3)
    inside = in_range(4 * p.chip - 2 + ii, 32)
    select = as_bf16(jnp.logical_and(inside, col == ii * 8 + jj))
    for n in range(CHUNKS):
        part = jnp.concatenate([a_rows[slot, 7 * p.c + n] for slot in range(4)], axis=0)
        a_perm[n * 64 : (n + 1) * 64, :] = jnp.dot(
            select, part, preferred_element_type=jnp.float32
        ).astype(jnp.bfloat16)


def arrange_b(p, b_rows, b_perm):
    for q in range(3):
        valid = in_range(p.rb - 1 + q, 16)
        for n in range(8):
            both = [b_rows[q, c, n].astype(jnp.float32) for c in range(2)]
            for k in range(2):
                rows16 = jnp.concatenate([v[8 * k : 8 * k + 8] for v in both], axis=0)
                b_perm[2 * q + k, 16 * n : 16 * n + 16, :] = jnp.where(
                    valid, rows16, 0.0
                ).astype(jnp.bfloat16)


J_STEP = 24
EDGE = 8


def correlate(p, a_perm, b_perm, patches):
    f32 = jnp.float32
    patches[pl.ds(CHUNKS * 8 * p.c, EDGE)] = jnp.zeros((EDGE, 9, 16, LANES), jnp.bfloat16)
    base = EDGE * (1 - p.c)
    for n in range(CHUNKS * 8 // J_STEP):
        part = a_perm[n * J_STEP * 8 : (n + 1) * J_STEP * 8, :]
        for pair in range(3):
            both = []
            for k in range(2):
                corr = lax.dot_general(
                    part, b_perm[2 * pair + k], (((1,), (1,)), ((), ())), preferred_element_type=f32
                )
                both.append(corr.reshape(J_STEP, 8, LANES))
            tile = jnp.concatenate(both, axis=1)
            for s in range(3):
                moved = tile if s == 1 else shifted(tile, s - 1)
                patches[pl.ds(base + n * J_STEP, J_STEP), s * 3 + pair] = moved.astype(jnp.bfloat16)


GROUP = 33
PAIRS = 33


def layers(p, patches, big1, bias_big, big2, hidden, taps):
    f32 = jnp.float32

    def one(n, _):
        for u in range(GROUP):
            j = (n * GROUP + u) * 2 + EDGE - 2
            left = patches[pl.ds(j, 3)].reshape(USED, LANES)
            right = patches[pl.ds(j + 1, 3)].reshape(USED, LANES)
            before = jnp.dot(
                big1[:, :USED], jnp.concatenate([left, right], axis=1), preferred_element_type=f32
            )
            bias = bias_big[...]
            hidden[u] = jnp.maximum(before + jnp.concatenate([bias, bias], axis=1), 0.0).astype(
                jnp.bfloat16
            )
        for u in range(GROUP):
            j = (n * GROUP + u) * 2
            out = jnp.dot(big2[...], hidden[u], preferred_element_type=f32)
            taps[j] = out[:, :LANES]
            taps[j + 1] = out[:, LANES:]
        return 0

    lax.fori_loop(0, PAIRS // GROUP, one, 0)
    taps[(2 * PAIRS - 1) * p.c] = jnp.zeros((72, LANES), f32)


def finish(taps, own, other):
    step = 16
    for n in range(HALF // step):
        start = n * step
        sums = []
        for d in range(3):
            total = None
            for b in range(3):
                row = (b * 3 + d) * 8
                part = taps[start + b : start + b + step, row : row + 8]
                total = part if total is None else total + part
            sums.append(total)
        value = sums[1] + shifted(sums[0], -1) + shifted(sums[2], 1)
        for i in range(2):
            rows = slice(2 * start, 2 * (start + step))
            own[i, rows] = value[:, 2 * i : 2 * i + 2].reshape(2 * step, LANES)
            other[i, rows] = value[:, 4 + 2 * i : 6 + 2 * i].reshape(2 * step, LANES)


def kernel(
    a_hbm, b_hbm, w1_hbm, bias1_hbm, w2_hbm,
    out_hbm,
    a_ref, b_ref, w1_ref, w2_ref, bias1_ref, load_sem,
    a_rows, b_rows, a_perm, b_perm, patches, taps, big1, bias_big, big2, hidden, own, other,
    send_sem, recv_sem,
):
    p = Place(lax.axis_index("ra"), lax.axis_index("rb"))
    barrier, count = greet(p)
    pairs = (
        (a_hbm, a_ref), (b_hbm, b_ref), (w1_hbm, w1_ref),
        (w2_hbm, w2_ref), (bias1_hbm, bias1_ref),
    )
    loads = [
        pltpu.make_async_copy(src, dst, load_sem.at[n]) for n, (src, dst) in enumerate(pairs)
    ]
    for load in loads:
        load.start()
    loads[0].wait()
    a_rows[1 + p.c, p.rb] = normalized(a_ref)
    loads[1].wait()
    b_rows[1, p.c, p.x * 2 + p.zh] = normalized(b_ref)
    pl.semaphore_wait(barrier, count)

    def meanwhile():
        for load in loads[2:]:
            load.wait()
        weights(p, w1_ref, bias1_ref, w2_ref, big1, bias_big, big2)

    def have_b():
        arrange_b(p, b_rows, b_perm)

    copies = gather(p, a_rows, b_rows, send_sem, recv_sem, meanwhile, have_b)
    arrange_a(p, a_rows, a_perm)
    correlate(p, a_perm, b_perm, patches)
    layers(p, patches, big1, bias_big, big2, hidden, taps)
    finish(taps, own, other)
    columns = pl.ds(2 * HALF * p.c, 2 * HALF)
    handed = copies.start(other, out_hbm.at[:, columns], p.mate)
    kept = pltpu.make_async_copy(own, out_hbm.at[:, columns], load_sem.at[0])
    kept.start()
    copies.wait_send()
    kept.wait()
    handed.wait_recv()
    assert len(copies.started) <= N_COPIES, len(copies.started)


def compute_scratch(channels):
    bf16, f32 = jnp.bfloat16, jnp.float32
    return [
        pltpu.VMEM((4, 16, 16, channels), bf16),
        pltpu.VMEM((3, 2, 8, 16, channels), bf16),
        pltpu.VMEM((CHUNKS * 64, channels), bf16),
        pltpu.VMEM((6, LANES, channels), bf16),
        pltpu.VMEM((CHUNKS * 8 + EDGE, 9, 16, LANES), bf16),
        pltpu.VMEM((2 * PAIRS, 72, LANES), f32),
        pltpu.VMEM((CELLS * HID, COLS), bf16),
        pltpu.VMEM((CELLS * HID, LANES), f32),
        pltpu.VMEM((72, CELLS * HID), bf16),
        pltpu.VMEM((GROUP, CELLS * HID, 256), bf16),
        pltpu.VMEM((2, 2 * HALF, LANES), f32),
        pltpu.VMEM((2, 2 * HALF, LANES), f32),
    ]


def per_device(features_a, features_b, weight_one, bias_one, weight_two, bias_two):
    channels = features_a.shape[-1]
    arguments = (features_a, features_b, weight_one, bias_one, weight_two)
    vmem = [pltpu.VMEM(v.shape, v.dtype) for v in (features_a, features_b, weight_one, weight_two)]
    smem = [pltpu.SMEM(v.shape, v.dtype) for v in (bias_one,)]
    rows = pl.pallas_call(
        kernel,
        out_shape=jax.ShapeDtypeStruct((2, 2 * LANES, LANES), jnp.float32),
        in_specs=[pl.BlockSpec(memory_space=pl.ANY)] * 5,
        out_specs=pl.BlockSpec(memory_space=pl.ANY),
        scratch_shapes=vmem
        + smem
        + [pltpu.SemaphoreType.DMA((5,))]
        + compute_scratch(channels)
        + [pltpu.SemaphoreType.DMA((N_COPIES,)), pltpu.SemaphoreType.DMA((N_COPIES + 4,))],
        compiler_params=pltpu.CompilerParams(
            collective_id=0, has_side_effects=True, vmem_limit_bytes=40 * 1024 * 1024
        ),
        name="consensus",
    )(*[pltpu.with_memory_space_constraint(v, pltpu.HBM) for v in arguments])
    return jax.nn.relu(rows.reshape(2, LANES, 2, LANES) + bias_two[0])


def solution(mesh):
    return jax.shard_map(
        per_device,
        mesh=mesh,
        in_specs=(P("ra", "rb", None), P("rb", "ra", None), P(), P(), P(), P()),
        out_specs=P("ra", None, "rb", None),
        check_vma=False,
    )
```
